128 devices in a mesh: row: 16 (over x, y_lo, core), col: 4 (over z), layer: 2 (over y_hi).
Axes of the slice: x: 4, y: 4 (y_hi: 2, y_lo: 2; y = y_hi * 2 + y_lo), z: 4, core: 2. Of those that a mesh axis runs over, the one named last changes fastest.
Arguments:
- a_blocks: bfloat16 [16, 4, 2, 12, 256, 256], P('row', 'col', 'layer'), may hold values from -6 to 6
- b_blocks: bfloat16 [16, 4, 2, 32, 256, 256], P('row', 'col', 'layer'), may hold values from -0.375 to 0.375
- a_offsets: int32 [24, 4, 12], P(None, 'col'), may hold values from -8 to 7, as said below
- b_offsets: int32 [256, 12], replicated, may hold values from -8 to 7, as said below
- keep_offsets: int32 [24, 4, 16], P(None, 'col', 'row'), may hold values from -16 to 15, as said below
- owners: int32 [24, 4, 16], P('layer', 'col', 'row'), may hold values from 0 to 3, as said below
Outputs:
- next_blocks: bfloat16 [16, 4, 2, 4, 6, 256, 256], P('row', 'col', 'layer')
The draws below stay inside these ranges and needn't reach their ends.
Inputs may be any that keep to these rules, and one draw needn't show every extreme that they name: `a_offsets`: the 12 offsets of each row are distinct. `b_offsets`: the 12 offsets of each row are distinct. keep_offsets[t, c, r] is congruent to r - c - 4 t modulo 16. Among the 12 values of owners[t, c, r] with t in one half [l * 12, (l + 1) * 12), at most 6 are equal; for every l and r one owner is named exactly 6 times for every c.
All inputs are finite; a program needn't handle non-finite values.
Results may differ from the reference program's by a relative error of at most 0.0042.
Values may be sent and summed in bfloat16 or wider, within the bound.
A program may use at most 192 MiB of HBM per device.

```python
import jax
import jax.numpy as jnp
from jax import lax

BLOCK = 256
SIDE_BLOCKS = 256
GROUP_ROWS = 24
BAND = 16
GROUPS = 4
LAYERS = 2
PIECES = 32
HELD_PIECES = 4
PIECE_ROWS = 8
SHARE_ROWS = 12
SEND_SLOTS = 6
ROW_BLOCKS = 12


def draw_a_offsets(key, part):
    key = jax.random.fold_in(key, 11)
    base = jnp.broadcast_to(jnp.arange(BAND, dtype=jnp.int32), (GROUP_ROWS, GROUPS, BAND))
    mixed = jax.random.permutation(key, base, axis=2, independent=True)
    return (mixed[:, :, :ROW_BLOCKS] - BAND // 2).astype(jnp.int32)


def draw_b_offsets(key, part):
    key = jax.random.fold_in(key, 12)
    base = jnp.broadcast_to(jnp.arange(BAND, dtype=jnp.int32), (SIDE_BLOCKS, BAND))
    mixed = jax.random.permutation(key, base, axis=1, independent=True)
    return (mixed[:, :ROW_BLOCKS] - BAND // 2).astype(jnp.int32)


def draw_keep_offsets(key, part):
    key = jax.random.fold_in(key, 13)
    tile_row = jnp.arange(GROUP_ROWS, dtype=jnp.int32)[:, None, None]
    group_index = jnp.arange(GROUPS, dtype=jnp.int32)[None, :, None]
    target = jnp.arange(BAND, dtype=jnp.int32)[None, None, :]
    lowest = jnp.remainder(target - group_index - GROUPS * tile_row, BAND) - BAND
    upper_side = jax.random.randint(key, (GROUP_ROWS, GROUPS, BAND), 0, 2)
    return (lowest + BAND * upper_side).astype(jnp.int32)


def draw_owners(key, part):
    key = jax.random.fold_in(key, 14)
    first, second, third = jax.random.split(key, 3)
    busiest = jax.random.randint(first, (LAYERS, 1, BAND, 1), 0, GROUPS)
    places = jnp.broadcast_to(jnp.arange(SHARE_ROWS, dtype=jnp.int32), (LAYERS, GROUPS, BAND, SHARE_ROWS))
    places = jax.random.permutation(second, places, axis=3, independent=True)
    others = jax.random.randint(third, (LAYERS, GROUPS, BAND, SHARE_ROWS), 1, GROUPS)
    chosen = jnp.where(places < SEND_SLOTS, busiest, jnp.remainder(busiest + others, GROUPS))
    return jnp.transpose(chosen, (0, 3, 1, 2)).reshape(GROUP_ROWS, GROUPS, BAND).astype(jnp.int32)


def levels(rng, dims, cuts, least, largest):
    loudness, own = 1.0, jax.random.fold_in(rng, 6)
    for axis_at, shards_of in cuts:
        draws = jnp.exp(jax.random.uniform(jax.random.fold_in(own, axis_at), (shards_of,), jnp.float32, least / len(cuts), largest / len(cuts)))
        loudness = loudness * jnp.repeat(draws, dims[axis_at] // shards_of).reshape([-1 if axis == axis_at else 1 for axis in range(len(dims))])
    return loudness


def normal_values(stream_key, extent, scale, limit, cuts=(), kind=jnp.bfloat16):
    values = jax.random.normal(stream_key, extent, jnp.float32) * scale
    if len(cuts) > 0:
        values = levels(stream_key, extent, cuts, -0.22, 0.18) * values
    return jnp.clip(values, min=-limit, max=limit).astype(kind)


def setup_inputs(seed: int = 0) -> dict:
    splits = jax.random.split(jax.random.key(seed), 7)
    return {
        "a_blocks": normal_values(splits[0], (BAND, GROUPS, LAYERS, SHARE_ROWS, BLOCK, BLOCK), 1.0, 6.0, ((0, 16), (1, 4), (2, 2))),
        "b_blocks": normal_values(splits[1], (BAND, GROUPS, LAYERS, HELD_PIECES * PIECE_ROWS, BLOCK, BLOCK), BLOCK ** -0.5, 0.375, ((0, 16), (1, 4), (2, 2))),
        "a_offsets": draw_a_offsets(jax.random.fold_in(splits[6], 71), 0),
        "b_offsets": draw_b_offsets(jax.random.fold_in(splits[6], 71), 0),
        "keep_offsets": draw_keep_offsets(jax.random.fold_in(splits[6], 71), 0),
        "owners": draw_owners(jax.random.fold_in(splits[6], 71), 0),
    }


def piece_plan(group_index, target, piece_id, row_offsets, b_offsets, kept_offsets, band_width, pieces, groups, held_pieces, group_rows, side_blocks):
    period = pieces // groups
    residues = jnp.arange(period, dtype=jnp.int32)
    inside = jnp.remainder(piece_id - group_index - groups * residues + band_width // 2, pieces) < band_width
    ranked = jnp.argsort(jnp.where(inside, residues, residues + period))[:held_pieces].astype(jnp.int32)
    periods = jnp.arange(group_rows // period, dtype=jnp.int32)
    tile_rows = (periods[:, None] * period + ranked[None, :]).reshape(-1)
    matrix_row = group_index + groups * tile_rows
    offset_a = jnp.remainder(piece_id - matrix_row + band_width // 2, pieces) - band_width // 2
    column_k = jnp.remainder(matrix_row + offset_a, side_blocks)
    piece_row = (column_k - piece_id) // pieces
    offset_b = jnp.remainder(target - column_k + band_width // 2, band_width) - band_width // 2
    a_present = jnp.any(row_offsets[tile_rows] == offset_a[:, None], axis=1)
    b_present = jnp.any(b_offsets[column_k] == offset_b[:, None], axis=1)
    kept_cell = kept_offsets[tile_rows] == offset_a + offset_b
    return tile_rows, piece_row.astype(jnp.int32), a_present & b_present & kept_cell


def tile_product(tile_index, a_blocks, b_blocks, a_offsets, b_offsets, keep_offsets):
    target = tile_index // GROUPS
    group_index = tile_index % GROUPS
    row_offsets = a_offsets[:, group_index, :]
    kept_offsets = keep_offsets[:, group_index, target]
    summed = jnp.zeros((GROUP_ROWS, BLOCK, BLOCK), jnp.float32)
    for layer_index in range(LAYERS):
        b_group = b_blocks[target, :, layer_index].reshape(GROUPS * HELD_PIECES * PIECE_ROWS, BLOCK, BLOCK)

        def one_step(piece_seq, total):
            piece_seq = jnp.asarray(piece_seq).astype(jnp.int32)
            source = jnp.remainder(piece_seq - HELD_PIECES * group_index, BAND)
            a_current = a_blocks[source, group_index, layer_index].astype(jnp.float32)
            distance = jnp.remainder(piece_seq - target, BAND)
            piece_id = (layer_index * BAND + piece_seq).astype(jnp.int32)
            tile_rows, piece_row, weight = piece_plan(group_index, target, piece_id, row_offsets, b_offsets, kept_offsets, BAND, PIECES, GROUPS, HELD_PIECES, GROUP_ROWS, SIDE_BLOCKS)
            chosen = b_group[distance * PIECE_ROWS + piece_row].astype(jnp.float32)
            products = jnp.einsum("sab,sbc->sac", a_current, chosen)
            return total.at[tile_rows].add(products * weight.astype(jnp.float32)[:, None, None])

        partial_value = lax.fori_loop(0, BAND, one_step, jnp.zeros((GROUP_ROWS, BLOCK, BLOCK), jnp.float32))
        rounded = lax.optimization_barrier(partial_value.astype(jnp.bfloat16))
        summed = summed + rounded.astype(jnp.float32)
    return summed.astype(jnp.bfloat16)


def reference(a_blocks, b_blocks, a_offsets, b_offsets, keep_offsets, owners):
    indices = jnp.arange(BAND * GROUPS, dtype=jnp.int32)
    tile_blocks = lax.map(lambda tile_index: tile_product(tile_index, a_blocks, b_blocks, a_offsets, b_offsets, keep_offsets), indices)
    tile_blocks = tile_blocks.reshape(BAND, GROUPS, GROUP_ROWS, BLOCK, BLOCK)
    owner_split = owners.reshape(LAYERS, SHARE_ROWS, GROUPS, BAND).astype(jnp.int32)
    one_hot = (owner_split[..., None] == jnp.arange(GROUPS, dtype=jnp.int32)).astype(jnp.int32)
    order_ranks = jnp.cumsum(one_hot, axis=1) - 1
    order_rank = jnp.take_along_axis(order_ranks, owner_split[..., None], axis=4)[..., 0].astype(jnp.int32)
    grid_layer, grid_share, grid_group, grid_target = jnp.meshgrid(jnp.arange(LAYERS, dtype=jnp.int32), jnp.arange(SHARE_ROWS, dtype=jnp.int32), jnp.arange(GROUPS, dtype=jnp.int32), jnp.arange(BAND, dtype=jnp.int32), indexing="ij")
    tile_row = grid_layer * SHARE_ROWS + grid_share
    result = jnp.zeros((BAND, GROUPS, LAYERS, GROUPS, SEND_SLOTS, BLOCK, BLOCK), jnp.bfloat16)
    result = result.at[grid_target, owner_split, grid_layer, grid_group, order_rank].set(tile_blocks[grid_target, grid_group, tile_row])
    return result
```

```python
import functools

import jax
import jax.numpy as jnp
from jax import lax
from jax.experimental import pallas as pl
from jax.experimental.pallas import tpu as pltpu
from jax.sharding import PartitionSpec as P

MESH = pl.DeviceIdType.MESH
BLOCK = 256
PHASES = 3
NX = 2


def mod(value, count):
    return lax.rem(value + 32 * count, jnp.int32(count))


def kernel(
    a_ref,
    b_ref,
    a_mask,
    b_mask,
    keep,
    slot_source,
    slot_used,
    out_ref,
    abuf,
    bbuf,
    total,
    mine,
    outgoing_part,
    incoming_part,
    slots,
    local_sem,
    a_send,
    b_send,
    p_send,
    o_send,
    x_recv,
    x2_recv,
    xy_recv,
    yy_recv,
    yx_recv,
    yx2_recv,
    core_recv,
    bz_recv,
    bz2_recv,
    p_recv,
    o_recv,
):
    r = lax.axis_index("row")
    c = lax.axis_index("col")
    l = lax.axis_index("layer")
    x, y, b = r // 4, (r // 2) % 2, r % 2

    def row_of(xx, yy, bb):
        return xx * 4 + yy * 2 + bb

    xp, xm, x2 = mod(x + 1, 4), mod(x - 1, 4), mod(x + 2, 4)
    zp, zm, z2 = mod(c + 1, 4), mod(c - 1, 4), mod(c + 2, 4)
    y1, b1, l1 = 1 - y, 1 - b, 1 - l
    to_xp, to_xm = {"row": row_of(xp, y, b)}, {"row": row_of(xm, y, b)}
    to_y, to_b = {"row": row_of(x, y1, b)}, {"row": row_of(x, y, b1)}
    to_zp, to_zm, to_z2 = {"col": zp}, {"col": zm}, {"col": z2}
    to_l = {"layer": l1}

    barrier = pltpu.get_barrier_semaphore()
    for device in (to_xp, to_xm, to_y, to_b, to_zp, to_zm, to_z2, to_l):
        pl.semaphore_signal(barrier, inc=1, device_id=device, device_id_type=MESH)
    pl.semaphore_wait(barrier, 8)

    def remote(src, dst, send, recv, device):
        return pltpu.make_async_remote_copy(
            src_ref=src, dst_ref=dst, send_sem=send, recv_sem=recv, device_id=device, device_id_type=MESH
        )

    def third(phase):
        return lax.rem(2 * phase, jnp.int32(3))

    def blocks(source, phase, first, count):
        return abuf.at[source, pl.ds(third(phase) * 4 + first, count)]

    def pass_a(source, phase, first, count, recv, device):
        ref = blocks(source, phase, first, count)
        remote(ref, ref, a_send.at[phase], recv, device).start()

    def got_a(source, phase, first, count, recv):
        ref = blocks(source, phase, first, count)
        remote(ref, ref, a_send.at[phase], recv, to_b).wait_recv()

    ny = 4 - NX
    half = NX // 2
    hy = ny // 2

    def own_copy(phase):
        return pltpu.make_async_copy(
            a_ref.at[pl.ds(third(phase) * 4, 4)], blocks(r, phase, 0, 4), local_sem.at[phase]
        )

    def b_own_copy(part):
        return pltpu.make_async_copy(
            b_ref.at[:, mod(part - l, 8)], bbuf.at[c, part], local_sem.at[PHASES + part]
        )

    def send_own(phase):
        own_copy(phase).wait()
        pass_a(r, phase, NX, ny, yy_recv.at[phase], to_y)
        pass_a(r, phase, 0, NX, x_recv.at[phase, 0], to_xp)
        pass_a(r, phase, 0, NX, x_recv.at[phase, 1], to_xm)
        pass_a(r, phase, NX, ny, yx_recv.at[phase, 0, 0], to_xp)
        pass_a(r, phase, NX, ny, yx_recv.at[phase, 0, 1], to_xm)
        pass_a(r, phase, 0, NX, xy_recv.at[phase, 0], to_y)
        pass_a(r, phase, 0, 4, core_recv.at[phase, 0], to_b)

    def pass_b(source, part, first, count, recv, device):
        ref = bbuf.at[source, part, pl.ds(first, count)]
        remote(ref, ref, b_send.at[part], recv, device).start()

    def got_b(source, part, first, count, recv):
        ref = bbuf.at[source, part, pl.ds(first, count)]
        remote(ref, ref, b_send.at[part], recv, to_zp).wait_recv()

    def send_own_b(part):
        b_own_copy(part).wait()
        pass_b(c, part, 0, 4, bz_recv.at[part, 0], to_zp)
        pass_b(c, part, 0, 4, bz_recv.at[part, 1], to_zm)

    def forward_b(part):
        got_b(zm, part, 0, 4, bz_recv.at[part, 0])
        pass_b(zm, part, 0, 2, bz2_recv.at[part, 0], to_zp)
        got_b(zp, part, 0, 4, bz_recv.at[part, 1])
        pass_b(zp, part, 2, 2, bz2_recv.at[part, 1], to_zm)

    def last_b(part):
        got_b(z2, part, 0, 2, bz2_recv.at[part, 0])
        got_b(z2, part, 2, 2, bz2_recv.at[part, 1])

    def multiply(source, phase):
        piece = 16 * l + mod(source + 4 * c, 16)
        top = mod(piece - c + 8, 32) // 4
        for g in range(4):
            u = jnp.where(top >= 3, top - 3 + g, jnp.where(g <= top, g, g + 4))
            t = 8 * third(phase) + u
            i = c + 4 * t
            d = mod(piece - i + 8, 32) - 8
            k = mod(i + d, 256)
            part = mod(k // 32 + l, 8)
            e = mod(r - k + 8, 16) - 8
            distance = mod(k - r, 16)
            present = (
                lax.shift_right_logical(a_mask[t], d + 8) & lax.shift_right_logical(b_mask[k], e + 8) & 1
            )
            weight = jnp.where(keep[t] == d + e, present, 0).astype(jnp.float32)
            product = jnp.dot(
                abuf[source, third(phase) * 4 + g],
                bbuf[distance // 4, part, distance % 4],
                preferred_element_type=jnp.float32,
            )
            total[u] += product * weight

    for phase in range(PHASES):
        own_copy(phase).start()
    for part in range(4):
        b_own_copy(part).start()
    send_own(0)
    send_own_b(0)
    send_own_b(1)

    def run_phase(phase, carry):
        s = row_of(x, y1, b)
        got_a(s, phase, NX, ny, yy_recv.at[phase])
        pass_a(s, phase, NX, ny, yx_recv.at[phase, 1, 0], to_xp)
        pass_a(s, phase, NX, ny, yx_recv.at[phase, 1, 1], to_xm)

        @pl.when(phase < 2)
        def _():
            part = 2 * phase
            forward_b(part)

        s = row_of(xm, y, b)
        got_a(s, phase, 0, NX, x_recv.at[phase, 0])
        pass_a(s, phase, 0, half, x2_recv.at[phase, 0], to_xp)
        pass_a(s, phase, 0, NX, xy_recv.at[phase, 1], to_y)
        s = row_of(xp, y, b)
        got_a(s, phase, 0, NX, x_recv.at[phase, 1])
        pass_a(s, phase, half, NX - half, x2_recv.at[phase, 1], to_xm)
        pass_a(s, phase, 0, NX, xy_recv.at[phase, 2], to_y)
        for index, yy in ((0, y), (1, y1)):
            s = row_of(xm, yy, b)
            got_a(s, phase, NX, ny, yx_recv.at[phase, index, 0])
            pass_a(s, phase, NX, hy, yx2_recv.at[phase, index, 0], to_xp)
            s = row_of(xp, yy, b)
            got_a(s, phase, NX, ny, yx_recv.at[phase, index, 1])
            pass_a(s, phase, NX + hy, ny - hy, yx2_recv.at[phase, index, 1], to_xm)

        @pl.when(phase < 2)
        def _():
            send_own(phase + 1)

        @pl.when(phase < 1)
        def _():
            send_own_b(2)
            send_own_b(3)

        s = row_of(x2, y, b)
        got_a(s, phase, 0, half, x2_recv.at[phase, 0])
        got_a(s, phase, half, NX - half, x2_recv.at[phase, 1])
        pass_a(s, phase, 0, NX, xy_recv.at[phase, 3], to_y)

        @pl.when(phase < 2)
        def _():
            part = 2 * phase
            forward_b(part + 1)

        pass_a(row_of(xm, y, b), phase, 0, 4, core_recv.at[phase, 1], to_b)
        pass_a(row_of(xp, y, b), phase, 0, 4, core_recv.at[phase, 2], to_b)
        for index in range(2):
            s = row_of(x2, (y, y1)[index], b)
            got_a(s, phase, NX, hy, yx2_recv.at[phase, index, 0])
            got_a(s, phase, NX + hy, ny - hy, yx2_recv.at[phase, index, 1])
        pass_a(row_of(x2, y, b), phase, 0, 4, core_recv.at[phase, 3], to_b)
        for index, xx in enumerate((x, xm, xp, x2)):
            s = row_of(xx, y1, b)
            got_a(s, phase, 0, NX, xy_recv.at[phase, index])
            pass_a(s, phase, 0, 4, core_recv.at[phase, 4 + index], to_b)

        @pl.when(phase < 2)
        def _():
            part = 2 * phase
            last_b(part)
            last_b(part + 1)

        for index, (xx, yy) in enumerate(
            ((x, y), (xm, y), (xp, y), (x2, y), (x, y1), (xm, y1), (xp, y1), (x2, y1))
        ):
            got_a(row_of(xx, yy, b1), phase, 0, 4, core_recv.at[phase, index])

        total[...] = jnp.zeros_like(total)

        def source_step(source, inner):
            multiply(source, phase)
            return inner

        lax.fori_loop(0, 16, source_step, 0)

        w = third(phase)

        def swap(first_mine, count, row_mine):
            def one(n, inner):
                mine[first_mine + n] = total[row_mine + n].astype(jnp.bfloat16)
                return inner

            lax.fori_loop(0, count, one, 0)

        def give(first, count, row, index):
            def one(n, inner):
                outgoing_part[first + n] = total[row + n].astype(jnp.bfloat16)
                return inner

            lax.fori_loop(0, count, one, 0)
            remote(
                outgoing_part.at[pl.ds(first, count)],
                incoming_part.at[pl.ds(first, count)],
                p_send.at[index],
                p_recv.at[index],
                to_l,
            ).start()

        @pl.when((w == 0) & (l == 0))
        def _():
            swap(0, 8, 0)

        @pl.when((w == 0) & (l == 1))
        def _():
            give(0, 8, 0, 0)

        @pl.when((w == 2) & (l == 1))
        def _():
            swap(4, 8, 0)

        @pl.when((w == 2) & (l == 0))
        def _():
            give(4, 8, 0, 0)

        @pl.when((w == 1) & (l == 0))
        def _():
            give(0, 4, 4, 1)
            swap(8, 4, 0)

        @pl.when((w == 1) & (l == 1))
        def _():
            give(8, 4, 0, 1)
            swap(0, 4, 4)

        return carry

    lax.fori_loop(0, PHASES, run_phase, 0)

    def part_copy(first, count, index):
        return remote(
            outgoing_part.at[pl.ds(first, count)],
            incoming_part.at[pl.ds(first, count)],
            p_send.at[index],
            p_recv.at[index],
            to_l,
        )

    @pl.when(l == 0)
    def _():
        part_copy(0, 8, 0).wait_recv()
        part_copy(8, 4, 1).wait_recv()

    @pl.when(l == 1)
    def _():
        part_copy(4, 8, 0).wait_recv()
        part_copy(0, 4, 1).wait_recv()

    def fill(owner):
        def one(n, inner):
            index = slot_source[owner * 6 + n]
            value = mine[index].astype(jnp.float32) + incoming_part[index].astype(jnp.float32)
            slots[owner, n] = (value * slot_used[owner * 6 + n].astype(jnp.float32)).astype(jnp.bfloat16)
            return inner

        lax.fori_loop(0, 6, one, 0)

    def slot_copy(owner, index, device):
        return remote(slots.at[owner], out_ref.at[c], o_send.at[index], o_recv.at[index], device)

    for index, (owner, device) in enumerate(((z2, to_z2), (zp, to_zp), (zm, to_zm))):
        fill(owner)
        slot_copy(owner, index, device).start()
    fill(c)
    stay = pltpu.make_async_copy(slots.at[c], out_ref.at[c], local_sem.at[PHASES + 4])
    stay.start()
    for phase in range(PHASES):
        ref = abuf.at[pl.ds(0, 5)]
        remote(ref, ref, a_send.at[phase], core_recv.at[phase, 0], to_b).wait_send()
    for part in range(4):
        ref = bbuf.at[pl.ds(0, 3), part]
        remote(ref, ref, b_send.at[part], bz_recv.at[part, 0], to_zp).wait_send()

    @pl.when(l == 0)
    def _():
        part_copy(4, 8, 0).wait_send()
        part_copy(0, 4, 1).wait_send()

    @pl.when(l == 1)
    def _():
        part_copy(0, 8, 0).wait_send()
        part_copy(8, 4, 1).wait_send()

    stay.wait()
    for index, (owner, device, sender) in enumerate(((z2, to_z2, z2), (zp, to_zp, zm), (zm, to_zm, zp))):
        slot_copy(owner, index, device).wait_send()
        remote(slots.at[owner], out_ref.at[sender], o_send.at[index], o_recv.at[index], device).wait_recv()


def on_device(a_blocks, b_blocks, a_offsets, b_offsets, keep_offsets, owners):
    a_part = a_blocks.reshape(12, BLOCK, BLOCK)
    b_part = b_blocks.reshape(4, 8, BLOCK, BLOCK)
    a_mask = jnp.sum(1 << (a_offsets[:, 0, :] + 8), axis=1)
    b_mask = jnp.sum(1 << (b_offsets + 8), axis=1)
    keep = keep_offsets[:, 0, 0]
    owner = owners[:, 0, 0]
    names = jnp.arange(4, dtype=jnp.int32)
    same = (owner[:, None] == owner[None, :]) & (jnp.arange(12)[:, None] > jnp.arange(12)[None, :])
    rank = jnp.sum(same.astype(jnp.int32), axis=1)
    chosen = (owner[None, None, :] == names[:, None, None]) & (
        rank[None, None, :] == jnp.arange(6, dtype=jnp.int32)[None, :, None]
    )
    slot_source = jnp.sum(chosen * jnp.arange(12, dtype=jnp.int32), axis=2).reshape(24)
    slot_used = jnp.sum(chosen.astype(jnp.int32), axis=2).reshape(24)
    smem = pl.BlockSpec(memory_space=pltpu.SMEM)
    anywhere = pl.BlockSpec(memory_space=pl.ANY)
    dma = pltpu.SemaphoreType.DMA
    block = (BLOCK, BLOCK)
    arrived = pl.pallas_call(
        kernel,
        out_shape=jax.ShapeDtypeStruct((4, 6, BLOCK, BLOCK), jnp.bfloat16),
        in_specs=[anywhere, anywhere, smem, smem, smem, smem, smem],
        out_specs=anywhere,
        scratch_shapes=[
            pltpu.VMEM((16, 12) + block, jnp.bfloat16),
            pltpu.VMEM((4, 4, 4) + block, jnp.bfloat16),
            pltpu.VMEM((8,) + block, jnp.float32),
            pltpu.VMEM((12,) + block, jnp.bfloat16),
            pltpu.VMEM((12,) + block, jnp.bfloat16),
            pltpu.VMEM((12,) + block, jnp.bfloat16),
            pltpu.VMEM((4, 6) + block, jnp.bfloat16),
            dma((PHASES + 5,)),
            dma((PHASES,)),
            dma((4,)),
            dma((2,)),
            dma((3,)),
            dma((PHASES, 2)),
            dma((PHASES, 2)),
            dma((PHASES, 4)),
            dma((PHASES,)),
            dma((PHASES, 2, 2)),
            dma((PHASES, 2, 2)),
            dma((PHASES, 8)),
            dma((4, 2)),
            dma((4, 2)),
            dma((2,)),
            dma((3,)),
        ],
        compiler_params=pltpu.CompilerParams(
            collective_id=0, has_side_effects=True, vmem_limit_bytes=56 << 20
        ),
        cost_estimate=pl.CostEstimate(
            flops=192 * 2 * BLOCK**3, bytes_accessed=10 << 20, transcendentals=0
        ),
        name="banded_product",
    )(a_part, b_part, a_mask, b_mask, keep, slot_source, slot_used)
    return arrived.reshape(1, 1, 1, 4, 6, BLOCK, BLOCK)


def solution(mesh):
    return jax.shard_map(
        on_device,
        mesh=mesh,
        in_specs=(
            P("row", "col", "layer", None, None, None),
            P("row", "col", "layer", None, None, None),
            P(None, "col", None),
            P(),
            P(None, "col", "row"),
            P("layer", "col", "row"),
        ),
        out_specs=P("row", "col", "layer", None, None, None, None),
        check_vma=False,
    )
```

```python
import functools

import jax
import jax.numpy as jnp
from jax import lax
from jax.experimental import pallas as pl
from jax.experimental.pallas import tpu as pltpu
from jax.sharding import PartitionSpec as P

MESH = pl.DeviceIdType.MESH
BLOCK = 256
PHASES = 3
NX = 1
NY = 3


def mod(value, count):
    return lax.rem(value + 32 * count, jnp.int32(count))


def kernel(
    a_ref,
    b_ref,
    a_mask,
    b_mask,
    keep,
    slot_source,
    slot_used,
    out_ref,
    abuf,
    bbuf,
    total,
    mine,
    outgoing_part,
    incoming_part,
    slots,
    local_sem,
    a_send,
    b_send,
    p_send,
    o_send,
    x_recv,
    x2_recv,
    xy_recv,
    yy_recv,
    yx_recv,
    yx2_recv,
    core_recv,
    bz_recv,
    bz2_recv,
    p_recv,
    o_recv,
    edge_send,
    edge_recv,
):
    r = lax.axis_index("row")
    c = lax.axis_index("col")
    l = lax.axis_index("layer")
    x, y, b = r // 4, (r // 2) % 2, r % 2

    def row_of(xx, yy, bb):
        return xx * 4 + yy * 2 + bb

    xp, xm, x2 = mod(x + 1, 4), mod(x - 1, 4), mod(x + 2, 4)
    zp, zm, z2 = mod(c + 1, 4), mod(c - 1, 4), mod(c + 2, 4)
    y1, b1, l1 = 1 - y, 1 - b, 1 - l
    to_xp, to_xm = {"row": row_of(xp, y, b)}, {"row": row_of(xm, y, b)}
    to_y, to_b = {"row": row_of(x, y1, b)}, {"row": row_of(x, y, b1)}
    to_zp, to_zm, to_z2 = {"col": zp}, {"col": zm}, {"col": z2}
    to_l = {"layer": l1}

    barrier = pltpu.get_barrier_semaphore()
    for device in (to_xp, to_xm, to_y, to_b, to_zp, to_zm, to_z2, to_l):
        pl.semaphore_signal(barrier, inc=1, device_id=device, device_id_type=MESH)
    pl.semaphore_wait(barrier, 8)

    def remote(src, dst, send, recv, device):
        return pltpu.make_async_remote_copy(
            src_ref=src, dst_ref=dst, send_sem=send, recv_sem=recv, device_id=device, device_id_type=MESH
        )

    def third(phase):
        return jnp.where(phase == 0, 2 * l1, jnp.where(phase == 1, 2 * l, 1))

    def blocks(source, phase, first, count):
        return abuf.at[source, pl.ds(third(phase) * 4 + first, count)]

    def pass_a(source, phase, first, count, recv, device):
        ref = blocks(source, phase, first, count)
        remote(ref, ref, a_send.at[phase], recv, device).start()

    def got_a(source, phase, first, count, recv):
        ref = blocks(source, phase, first, count)
        remote(ref, ref, a_send.at[phase], recv, to_b).wait_recv()

    def own_copy(phase):
        return pltpu.make_async_copy(
            a_ref.at[pl.ds(third(phase) * 4, 4)], blocks(r, phase, 0, 4), local_sem.at[phase]
        )

    def b_own_copy(part):
        return pltpu.make_async_copy(
            b_ref.at[:, mod(part - l, 8)], bbuf.at[c, part], local_sem.at[PHASES + part]
        )

    def send_own(phase):
        own_copy(phase).wait()
        pass_a(r, phase, NX, NY, yy_recv.at[phase], to_y)
        pass_a(r, phase, 0, NX, x_recv.at[phase, 0], to_xp)
        pass_a(r, phase, 0, NX, x_recv.at[phase, 1], to_xm)
        pass_a(r, phase, NX, NY, yx_recv.at[phase, 0, 0], to_xp)
        pass_a(r, phase, NX, NY, yx_recv.at[phase, 0, 1], to_xm)
        pass_a(r, phase, 0, NX, xy_recv.at[phase, 0], to_y)

    def pass_b(source, part, first, count, recv, device):
        ref = bbuf.at[source, part, pl.ds(first, count)]
        remote(ref, ref, b_send.at[part], recv, device).start()

    def got_b(source, part, first, count, recv):
        ref = bbuf.at[source, part, pl.ds(first, count)]
        remote(ref, ref, b_send.at[part], recv, to_zp).wait_recv()

    def send_own_b(part):
        b_own_copy(part).wait()
        pass_b(c, part, 0, 4, bz_recv.at[part, 0], to_zp)
        pass_b(c, part, 0, 4, bz_recv.at[part, 1], to_zm)

    def forward_b(part):
        got_b(zm, part, 0, 4, bz_recv.at[part, 0])
        pass_b(zm, part, 0, 2, bz2_recv.at[part, 0], to_zp)
        got_b(zp, part, 0, 4, bz_recv.at[part, 1])
        pass_b(zp, part, 2, 2, bz2_recv.at[part, 1], to_zm)

    def last_b(part):
        got_b(z2, part, 0, 2, bz2_recv.at[part, 0])
        got_b(z2, part, 2, 2, bz2_recv.at[part, 1])

    edge = 3 * l1
    middle = 2 - l

    def inside(source, n):
        q = mod(r + 4 * source + n, 16)
        return jnp.where(l == 0, jnp.where(q <= 6, 1, 0), jnp.where(q >= 8, 1, 0)) == 1

    def edge_copy(source, n, send, recv, device):
        ref = bbuf.at[source, edge, n]
        return remote(ref, ref, edge_send.at[send, n], edge_recv.at[recv, n], device)

    def send_own_edge():
        b_own_copy(edge).wait()
        for n in range(4):

            @pl.when(inside(c, n))
            def _():
                edge_copy(c, n, 0, 0, to_zp).start()
                edge_copy(c, n, 1, 1, to_zm).start()

    def forward_edge():
        for n in range(4):

            @pl.when(inside(zm, n))
            def _():
                edge_copy(zm, n, 0, 0, to_zp).wait_recv()
                if n < 2:
                    edge_copy(zm, n, 2, 2, to_zp).start()

            @pl.when(inside(zp, n))
            def _():
                edge_copy(zp, n, 1, 1, to_zm).wait_recv()
                if n >= 2:
                    edge_copy(zp, n, 2, 2, to_zm).start()

    def last_edge():
        for n in range(4):

            @pl.when(inside(z2, n))
            def _():
                edge_copy(z2, n, 2, 2, to_zp).wait_recv()

    def sent_edge():
        for n in range(4):

            @pl.when(inside(c, n))
            def _():
                edge_copy(c, n, 0, 0, to_zp).wait_send()
                edge_copy(c, n, 1, 1, to_zm).wait_send()

            @pl.when(inside(zm if n < 2 else zp, n))
            def _():
                edge_copy(c, n, 2, 2, to_zp).wait_send()

    def multiply(source, phase):
        piece = 16 * l + mod(source + 4 * c, 16)
        top = mod(piece - c + 8, 32) // 4
        for g in range(4):
            u = jnp.where(top >= 3, top - 3 + g, jnp.where(g <= top, g, g + 4))
            t = 8 * third(phase) + u
            i = c + 4 * t
            d = mod(piece - i + 8, 32) - 8
            k = mod(i + d, 256)
            part = mod(k // 32 + l, 8)
            e = mod(r - k + 8, 16) - 8
            distance = mod(k - r, 16)
            present = (
                lax.shift_right_logical(a_mask[t], d + 8) & lax.shift_right_logical(b_mask[k], e + 8) & 1
            )
            weight = jnp.where(keep[t] == d + e, present, 0).astype(jnp.float32)
            product = jnp.dot(
                abuf[source, third(phase) * 4 + g],
                bbuf[distance // 4, part, distance % 4],
                preferred_element_type=jnp.float32,
            )
            total[u] += product * weight

    own_copy(0).start()
    b_own_copy(edge).start()
    b_own_copy(middle).start()
    own_copy(1).start()
    b_own_copy(2 * l).start()
    b_own_copy(2 * l + 1).start()
    own_copy(2).start()
    send_own(0)
    send_own_b(middle)
    send_own_edge()
    pass_a(r, 0, 0, 4, core_recv.at[0, 0], to_b)
    send_own(1)

    def send_on(phase):
        s = row_of(x, y1, b)
        got_a(s, phase, NX, NY, yy_recv.at[phase])
        pass_a(s, phase, NX, NY, yx_recv.at[phase, 1, 0], to_xp)
        pass_a(s, phase, NX, NY, yx_recv.at[phase, 1, 1], to_xm)

        s = row_of(xp, y, b)
        got_a(s, phase, 0, NX, x_recv.at[phase, 1])
        pass_a(s, phase, 0, NX, xy_recv.at[phase, 1], to_y)

        @pl.when(b == 1)
        def _():
            pass_a(row_of(xp, y, b), phase, 0, NX, x2_recv.at[phase], to_xm)

        s = row_of(xm, y, b)
        got_a(s, phase, 0, NX, x_recv.at[phase, 0])
        pass_a(s, phase, 0, NX, xy_recv.at[phase, 3], to_y)

        @pl.when(b == 0)
        def _():
            pass_a(row_of(xm, y, b), phase, 0, NX, x2_recv.at[phase], to_xp)

        for index, yy in ((0, y), (1, y1)):
            split = 1 + index
            s = row_of(xm, yy, b)
            got_a(s, phase, NX, NY, yx_recv.at[phase, index, 0])
            pass_a(s, phase, NX, split, yx2_recv.at[phase, index, 0], to_xp)
            s = row_of(xp, yy, b)
            got_a(s, phase, NX, NY, yx_recv.at[phase, index, 1])
            pass_a(s, phase, NX + split, NY - split, yx2_recv.at[phase, index, 1], to_xm)

        s = row_of(x2, y, b)
        got_a(s, phase, 0, NX, x2_recv.at[phase])
        pass_a(s, phase, 0, NX, xy_recv.at[phase, 2], to_y)
        for n in (1, 3):
            pass_a(row_of(mod(x + n, 4), y, b), phase, 0, 4, core_recv.at[phase, n], to_b)

    send_on(0)
    send_own(2)
    forward_b(middle)
    forward_edge()
    send_own_b(2 * l)
    send_own_b(2 * l + 1)

    def run_phase(phase, carry):
        @pl.when(phase < 2)
        def _():
            send_on(phase + 1)

        @pl.when(phase == 1)
        def _():
            forward_b(2 * l)
            forward_b(2 * l + 1)

        for index in range(2):
            split = 1 + index
            s = row_of(x2, (y, y1)[index], b)
            got_a(s, phase, NX, split, yx2_recv.at[phase, index, 0])
            got_a(s, phase, NX + split, NY - split, yx2_recv.at[phase, index, 1])
        pass_a(row_of(x2, y, b), phase, 0, 4, core_recv.at[phase, 2], to_b)
        for n in (0, 1, 3, 2):
            s = row_of(mod(x + n, 4), y1, b)
            got_a(s, phase, 0, NX, xy_recv.at[phase, n])
            pass_a(s, phase, 0, 4, core_recv.at[phase, 4 + n], to_b)

        @pl.when(phase == 0)
        def _():
            last_b(middle)
            last_edge()

        @pl.when(phase == 1)
        def _():
            last_b(2 * l)
            last_b(2 * l + 1)

        @pl.when(phase < 2)
        def _():
            pass_a(r, phase + 1, 0, 4, core_recv.at[phase + 1, 0], to_b)

        total[...] = jnp.zeros_like(total)

        def of_this_core(n, inner):
            multiply(row_of(mod(x + n, 4), mod(y + n // 4, 2), b), phase)
            return inner

        lax.fori_loop(0, 8, of_this_core, 0)

        def of_sibling(n, inner):
            source = row_of(mod(x + n, 4), mod(y + n // 4, 2), b1)
            got_a(source, phase, 0, 4, core_recv.at[phase, n])
            multiply(source, phase)
            return inner

        lax.fori_loop(0, 8, of_sibling, 0)

        def stay_here(first, count, row):
            def one(n, inner):
                mine[first + n] = total[row + n].astype(jnp.bfloat16)
                return inner

            lax.fori_loop(0, count, one, 0)

        def give(first, count, row, index):
            def one(n, inner):
                outgoing_part[first + n] = total[row + n].astype(jnp.bfloat16)
                return inner

            lax.fori_loop(0, count, one, 0)
            part_copy(first, count, index).start()

        @pl.when(phase == 0)
        def _():
            give(4 * l1, 8, 0, 0)

        @pl.when(phase == 1)
        def _():
            stay_here(4 * l, 8, 0)

        @pl.when(phase == 2)
        def _():
            give(8 * l, 4, 4 * l1, 1)
            stay_here(8 * l1, 4, 4 * l)

        return carry

    def part_copy(first, count, index):
        return remote(
            outgoing_part.at[pl.ds(first, count)],
            incoming_part.at[pl.ds(first, count)],
            p_send.at[index],
            p_recv.at[index],
            to_l,
        )

    lax.fori_loop(0, PHASES, run_phase, 0)

    part_copy(4 * l, 8, 0).wait_recv()
    part_copy(8 * l1, 4, 1).wait_recv()

    def fill(owner):
        def one(n, inner):
            index = slot_source[owner * 6 + n]
            value = mine[index].astype(jnp.float32) + incoming_part[index].astype(jnp.float32)
            slots[owner, n] = (value * slot_used[owner * 6 + n].astype(jnp.float32)).astype(jnp.bfloat16)
            return inner

        lax.fori_loop(0, 6, one, 0)

    def slot_copy(owner, index, device):
        return remote(slots.at[owner], out_ref.at[c], o_send.at[index], o_recv.at[index], device)

    for index, (owner, device) in enumerate(((z2, to_z2), (zp, to_zp), (zm, to_zm))):
        fill(owner)
        slot_copy(owner, index, device).start()
    fill(c)
    stay = pltpu.make_async_copy(slots.at[c], out_ref.at[c], local_sem.at[PHASES + 4])
    stay.start()
    for phase in range(PHASES):
        ref = abuf.at[pl.ds(0, 5)]
        remote(ref, ref, a_send.at[phase], core_recv.at[phase, 0], to_b).wait_send()
    for part in (middle, 2 * l, 2 * l + 1):
        ref = bbuf.at[pl.ds(0, 3), part]
        remote(ref, ref, b_send.at[part], bz_recv.at[part, 0], to_zp).wait_send()
    sent_edge()
    part_copy(4 * l1, 8, 0).wait_send()
    part_copy(8 * l, 4, 1).wait_send()
    stay.wait()
    for index, (owner, device, sender) in enumerate(((z2, to_z2, z2), (zp, to_zp, zm), (zm, to_zm, zp))):
        slot_copy(owner, index, device).wait_send()
        remote(slots.at[owner], out_ref.at[sender], o_send.at[index], o_recv.at[index], device).wait_recv()


def on_device(a_blocks, b_blocks, a_offsets, b_offsets, keep_offsets, owners):
    a_part = a_blocks.reshape(12, BLOCK, BLOCK)
    b_part = b_blocks.reshape(4, 8, BLOCK, BLOCK)
    a_mask = jnp.sum(1 << (a_offsets[:, 0, :] + 8), axis=1)
    b_mask = jnp.sum(1 << (b_offsets + 8), axis=1)
    keep = keep_offsets[:, 0, 0]
    owner = owners[:, 0, 0]
    names = jnp.arange(4, dtype=jnp.int32)
    same = (owner[:, None] == owner[None, :]) & (jnp.arange(12)[:, None] > jnp.arange(12)[None, :])
    rank = jnp.sum(same.astype(jnp.int32), axis=1)
    chosen = (owner[None, None, :] == names[:, None, None]) & (
        rank[None, None, :] == jnp.arange(6, dtype=jnp.int32)[None, :, None]
    )
    slot_source = jnp.sum(chosen * jnp.arange(12, dtype=jnp.int32), axis=2).reshape(24)
    slot_used = jnp.sum(chosen.astype(jnp.int32), axis=2).reshape(24)
    smem = pl.BlockSpec(memory_space=pltpu.SMEM)
    anywhere = pl.BlockSpec(memory_space=pl.ANY)
    dma = pltpu.SemaphoreType.DMA
    block = (BLOCK, BLOCK)
    arrived = pl.pallas_call(
        kernel,
        out_shape=jax.ShapeDtypeStruct((4, 6, BLOCK, BLOCK), jnp.bfloat16),
        in_specs=[anywhere, anywhere, smem, smem, smem, smem, smem],
        out_specs=anywhere,
        scratch_shapes=[
            pltpu.VMEM((16, 12) + block, jnp.bfloat16),
            pltpu.VMEM((4, 4, 4) + block, jnp.bfloat16),
            pltpu.VMEM((8,) + block, jnp.float32),
            pltpu.VMEM((12,) + block, jnp.bfloat16),
            pltpu.VMEM((12,) + block, jnp.bfloat16),
            pltpu.VMEM((12,) + block, jnp.bfloat16),
            pltpu.VMEM((4, 6) + block, jnp.bfloat16),
            dma((PHASES + 5,)),
            dma((PHASES,)),
            dma((4,)),
            dma((2,)),
            dma((3,)),
            dma((PHASES, 2)),
            dma((PHASES,)),
            dma((PHASES, 4)),
            dma((PHASES,)),
            dma((PHASES, 2, 2)),
            dma((PHASES, 2, 2)),
            dma((PHASES, 8)),
            dma((4, 2)),
            dma((4, 2)),
            dma((2,)),
            dma((3,)),
            dma((3, 4)),
            dma((3, 4)),
        ],
        compiler_params=pltpu.CompilerParams(
            collective_id=0, has_side_effects=True, vmem_limit_bytes=56 << 20
        ),
        cost_estimate=pl.CostEstimate(
            flops=192 * 2 * BLOCK**3, bytes_accessed=10 << 20, transcendentals=0
        ),
        name="banded_product",
    )(a_part, b_part, a_mask, b_mask, keep, slot_source, slot_used)
    return arrived.reshape(1, 1, 1, 4, 6, BLOCK, BLOCK)


def solution(mesh):
    return jax.shard_map(
        on_device,
        mesh=mesh,
        in_specs=(
            P("row", "col", "layer", None, None, None),
            P("row", "col", "layer", None, None, None),
            P(None, "col", None),
            P(),
            P(None, "col", "row"),
            P("layer", "col", "row"),
        ),
        out_specs=P("row", "col", "layer", None, None, None, None),
        check_vma=False,
    )
```

```python
import functools

import jax
import jax.numpy as jnp
from jax import lax
from jax.experimental import pallas as pl
from jax.experimental.pallas import tpu as pltpu
from jax.sharding import PartitionSpec as P

MESH = pl.DeviceIdType.MESH
BLOCK = 256


def mod(value, count):
    return lax.rem(value + 32 * count, jnp.int32(count))


def kernel(
    a_ref,
    b_ref,
    a_offsets,
    b_offsets,
    keep,
    owners,
    keep_vector,
    out_ref,
    abuf,
    bbuf,
    total,
    parts,
    leaving,
    swapped,
    slots,
    keep_arrived,
    keep_other,
    a_mask,
    b_mask,
    rank,
    slot_source,
    slot_used,
    local_sem,
    keep_sem,
    a_send,
    yy_recv,
    yx_recv,
    yx2_recv,
    core_recv,
    by_send,
    by_recv,
    bz_send,
    bz_recv,
    p_send,
    p_recv,
    o_send,
    o_recv,
):
    r = lax.axis_index("row")
    c = lax.axis_index("col")
    l = lax.axis_index("layer")
    x, y, b = r // 4, (r // 2) % 2, r % 2

    def row_of(xx, yy, bb):
        return xx * 4 + yy * 2 + bb

    xp, xm, x2 = mod(x + 1, 4), mod(x - 1, 4), mod(x + 2, 4)
    zp, zm, z2 = mod(c + 1, 4), mod(c - 1, 4), mod(c + 2, 4)
    y1, b1, l1 = 1 - y, 1 - b, 1 - l
    r1 = row_of(x, y1, b)
    to_xp, to_xm = {"row": row_of(xp, y, b)}, {"row": row_of(xm, y, b)}
    to_y, to_b = {"row": r1}, {"row": row_of(x, y, b1)}
    to_zp, to_zm, to_z2 = {"col": zp}, {"col": zm}, {"col": z2}
    to_l, to_yl = {"layer": l1}, {"row": r1, "layer": l1}

    barrier = pltpu.get_barrier_semaphore()
    for device in (to_xp, to_xm, to_y, to_b, to_zp, to_zm, to_z2, to_l, to_yl):
        pl.semaphore_signal(barrier, inc=1, device_id=device, device_id_type=MESH)
    pl.semaphore_wait(barrier, 9)

    def remote(src, dst, send, recv, device):
        return pltpu.make_async_remote_copy(
            src_ref=src, dst_ref=dst, send_sem=send, recv_sem=recv, device_id=device, device_id_type=MESH
        )

    def third(phase):
        return 2 * y if phase == 0 else 1

    def pass_a(source, phase, first, count, recv, device):
        ref = abuf.at[phase, source, pl.ds(first, count)]
        remote(ref, ref, a_send.at[phase], recv, device).start()

    def got_a(source, phase, first, count, recv):
        ref = abuf.at[phase, source, pl.ds(first, count)]
        remote(ref, ref, a_send.at[phase], recv, to_b).wait_recv()

    def own_copy(phase):
        return pltpu.make_async_copy(
            a_ref.at[pl.ds(third(phase) * 4, 4)], abuf.at[phase, r], local_sem.at[phase]
        )

    def a_to_y(phase):
        first = 8 * y1 if phase == 0 else 4
        remote(
            a_ref.at[pl.ds(first, 4)], abuf.at[phase, r], a_send.at[phase], yy_recv.at[phase], to_y
        ).start()

    def a_along_x(phase, yy):
        index = 0 if yy is y else 1
        s = row_of(x, yy, b)
        pass_a(s, phase, 0, 4, yx_recv.at[phase, index, 0], to_xp)
        pass_a(s, phase, 0, 4, yx_recv.at[phase, index, 1], to_xm)

    def a_further(phase, yy):
        index = 0 if yy is y else 1
        s = row_of(xm, yy, b)
        got_a(s, phase, 0, 4, yx_recv.at[phase, index, 0])
        pass_a(s, phase, 0, 2, yx2_recv.at[phase, index, 0], to_xp)
        s = row_of(xp, yy, b)
        got_a(s, phase, 0, 4, yx_recv.at[phase, index, 1])
        pass_a(s, phase, 2, 2, yx2_recv.at[phase, index, 1], to_xm)

    def to_sibling(phase, n):
        source = row_of(mod(x + n, 4), mod(y + n // 4, 2), b)
        pass_a(source, phase, 0, 4, core_recv.at[phase, n], to_b)

    def a_last(phase, yy):
        index = 0 if yy is y else 1
        s = row_of(x2, yy, b)
        got_a(s, phase, 0, 2, yx2_recv.at[phase, index, 0])
        got_a(s, phase, 2, 2, yx2_recv.at[phase, index, 1])

    other_full, other_edge = 3 + l, 4 - l
    own_second, own_last = 2 * y, 2 - 2 * y

    def b_own_copy(part):
        return pltpu.make_async_copy(
            b_ref.at[:, mod(y + part - l, 8)], bbuf.at[part, c], local_sem.at[2 + part]
        )

    def b_full_over_y():
        return remote(
            b_ref.at[:, mod(2 * y1, 8)], bbuf.at[other_full, c], by_send.at[4], by_recv.at[4], to_y
        )

    def b_edge_over_y(n):
        return remote(
            b_ref.at[n, mod(2 * y1 + 1 - 2 * l, 8)],
            bbuf.at[other_edge, c, n],
            by_send.at[n],
            by_recv.at[n],
            to_y,
        )

    def near(column, source, n):
        q = mod(column + 4 * source + n, 16)
        return jnp.where(l == 0, jnp.where(q <= 6, 1, 0), jnp.where(q >= 8, 1, 0))

    def edges_over_y(column, act):
        for n in range(4):

            @pl.when(near(column, c, n) == 1)
            def _():
                act(b_edge_over_y(n))

    def inside(part, source, n):
        column = jnp.where(part >= 3, r1, r)
        whole = jnp.where(part >= 3, jnp.where(part == other_full, 1, 0), jnp.where(part == 2 * l1, 0, 1))
        return whole + near(column, source, n) > 0

    def b_copy(part, source, n, way, device):
        ref = bbuf.at[part, source, n]
        return remote(ref, ref, bz_send.at[way, part, n], bz_recv.at[way, part, n], device)

    def b_start(part):
        for n in range(4):

            @pl.when(inside(part, c, n))
            def _():
                b_copy(part, c, n, 0, to_zp).start()
                b_copy(part, c, n, 1, to_zm).start()

    def b_further(part):
        for n in range(4):

            @pl.when(inside(part, zm, n))
            def _():
                b_copy(part, zm, n, 0, to_zp).wait_recv()
                if n < 2:
                    b_copy(part, zm, n, 2, to_zp).start()

            @pl.when(inside(part, zp, n))
            def _():
                b_copy(part, zp, n, 1, to_zm).wait_recv()
                if n >= 2:
                    b_copy(part, zp, n, 2, to_zm).start()

    def b_last(part):
        for n in range(4):

            @pl.when(inside(part, z2, n))
            def _():
                b_copy(part, z2, n, 2, to_zp).wait_recv()

    def b_sent(part):
        for n in range(4):

            @pl.when(inside(part, c, n))
            def _():
                b_copy(part, c, n, 0, to_zp).wait_send()
                b_copy(part, c, n, 1, to_zm).wait_send()

            @pl.when(inside(part, zm if n < 2 else zp, n))
            def _():
                b_copy(part, c, n, 2, to_zp).wait_send()

    def multiply(source, phase, column, keeps, first_part):
        piece = 16 * l + mod(source + 4 * c, 16)
        top = mod(piece - c + 8, 32) // 4
        for g in range(4):
            u = jnp.where(top >= 3, top - 3 + g, jnp.where(g <= top, g, g + 4))
            t = 8 * third(phase) + u
            i = c + 4 * t
            d = mod(piece - i + 8, 32) - 8
            k = mod(i + d, 256)
            part = mod(k // 32 + l, 8) + first_part
            e = mod(column - k + 8, 16) - 8
            distance = mod(k - column, 16)
            present = (
                lax.shift_right_logical(a_mask[t], d + 8) & lax.shift_right_logical(b_mask[k], e + 8) & 1
            )
            weight = jnp.where(keeps(t) == d + e, present, 0).astype(jnp.float32)
            product = jnp.dot(
                abuf[phase, source, g],
                bbuf[part, distance // 4, distance % 4],
                preferred_element_type=jnp.float32,
            )
            total[u] += product * weight

    def own_keep(t):
        return keep[t]

    def other_keep(t):
        return keep_other[0, t]

    def add_sources(phase, column, keeps, first_part, wait):
        total[...] = jnp.zeros_like(total)

        def of_this_core(n, inner):
            multiply(row_of(mod(x + n, 4), mod(y + n // 4, 2), b), phase, column, keeps, first_part)
            return inner

        lax.fori_loop(0, 8, of_this_core, 0)

        def of_sibling(n, inner):
            source = row_of(mod(x + n, 4), mod(y + n // 4, 2), b1)
            if wait:
                got_a(source, phase, 0, 4, core_recv.at[phase, n])
            multiply(source, phase, column, keeps, first_part)
            return inner

        lax.fori_loop(0, 8, of_sibling, 0)

    def store_rows(put, count, row):
        def one(n, inner):
            put(n, total[row + n].astype(jnp.bfloat16))
            return inner

        lax.fori_loop(0, count, one, 0)

    def column_copy(index, device):
        return remote(
            leaving.at[index],
            parts.at[l, pl.ds(4 * y, 8)],
            p_send.at[index],
            p_recv.at[l],
            device,
        )

    to_other_column = {"row": r1, "layer": y}

    def middle_copy():
        return remote(swapped, parts.at[l, pl.ds(8 * l, 4)], p_send.at[2], p_recv.at[2], to_l)

    def bits(offsets, at):
        found = jnp.int32(0)
        for n in range(12):
            found += lax.shift_left(jnp.int32(1), offsets[n, at] + 8)
        return found

    def plan():
        def a_row(t, inner):
            a_mask[t] = bits(a_offsets, t)
            return inner

        lax.fori_loop(0, 24, a_row, 0)

        def b_row(n, inner):
            k = mod(n - 8, 256)
            b_mask[k] = bits(b_offsets, k)
            return inner

        lax.fori_loop(0, 111, b_row, 0)
        for t in range(12):
            before = jnp.int32(0)
            for n in range(t):
                before += jnp.where(owners[n] == owners[t], 1, 0)
            rank[t] = before

        def slot(at, inner):
            owner, place = at // 6, at % 6
            source, used = jnp.int32(0), jnp.int32(0)
            for t in range(12):
                here = jnp.where((owners[t] == owner) & (rank[t] == place), 1, 0)
                source += here * t
                used += here
            slot_source[at] = source
            slot_used[at] = used
            return inner

        lax.fori_loop(0, 24, slot, 0)

    own_copy(0).start()
    b_own_copy(1).start()
    b_own_copy(own_second).start()
    own_copy(1).start()
    b_own_copy(own_last).start()
    a_to_y(0)
    b_full_over_y().start()
    keep_copy = remote(keep_vector, keep_arrived, keep_sem.at[0], keep_sem.at[1], to_y)
    keep_copy.start()
    own_copy(0).wait()
    a_along_x(0, y)
    b_own_copy(1).wait()
    b_start(1)
    b_own_copy(own_second).wait()
    b_start(own_second)
    own_copy(1).wait()
    a_along_x(1, y)
    to_sibling(0, 0)
    plan()
    got_a(r1, 0, 0, 4, yy_recv.at[0])
    a_along_x(0, y1)
    edges_over_y(r, lambda copy: copy.start())
    b_full_over_y().wait_recv()
    b_start(other_full)
    a_to_y(1)
    to_sibling(0, 4)
    a_further(0, y)
    b_further(1)
    to_sibling(0, 1)
    to_sibling(0, 3)
    b_further(own_second)
    edges_over_y(r1, lambda copy: copy.wait_recv())
    b_start(other_edge)
    a_further(0, y1)
    to_sibling(0, 5)
    to_sibling(0, 7)
    got_a(r1, 1, 0, 4, yy_recv.at[1])
    a_along_x(1, y1)
    b_further(other_full)
    b_own_copy(own_last).wait()
    b_start(own_last)
    a_further(1, y)
    a_last(0, y)
    to_sibling(0, 2)
    a_last(0, y1)
    to_sibling(0, 6)
    to_sibling(1, 0)
    to_sibling(1, 4)
    b_last(1)
    b_last(own_second)
    b_further(other_edge)
    add_sources(0, r, own_keep, -y, True)

    @pl.when(y == l)
    def _():
        def put_here(n, value):
            parts[l, 4 * y + n] = value

        store_rows(put_here, 8, 0)

    @pl.when(y != l)
    def _():
        def put_own(n, value):
            leaving[1, n] = value

        store_rows(put_own, 8, 0)
        column_copy(1, to_l).start()

    to_sibling(1, 1)
    to_sibling(1, 3)
    a_further(1, y1)
    to_sibling(1, 5)
    to_sibling(1, 7)
    b_further(own_last)
    keep_copy.wait_recv()
    keep_local = pltpu.make_async_copy(keep_arrived, keep_other, local_sem.at[6])
    keep_local.start()
    keep_local.wait()
    b_last(other_full)
    b_last(other_edge)
    add_sources(0, r1, other_keep, 3 - 2 * y, False)

    def put_other(n, value):
        leaving[0, n] = value

    store_rows(put_other, 8, 0)
    column_copy(0, to_other_column).start()

    a_last(1, y)
    to_sibling(1, 2)
    a_last(1, y1)
    to_sibling(1, 6)
    b_last(own_last)
    add_sources(1, r, own_keep, -y, True)

    def put_middle(n, value):
        swapped[n] = value

    store_rows(put_middle, 4, 4 * l1)
    middle_copy().start()

    def put_middle_here(n, value):
        parts[l, 8 * l1 + n] = value

    store_rows(put_middle_here, 4, 4 * l)

    def part_arrived(layer):
        ref = parts.at[layer, pl.ds(4 * l, 8)]
        remote(leaving.at[0], ref, p_send.at[0], p_recv.at[layer], to_l).wait_recv()

    @pl.when(y == l)
    def _():
        part_arrived(l1)

    @pl.when(y != l)
    def _():
        part_arrived(0)
        part_arrived(1)

    remote(swapped, parts.at[l1, pl.ds(8 * l1, 4)], p_send.at[2], p_recv.at[2], to_l).wait_recv()

    def fill(owner):
        def one(n, inner):
            index = slot_source[owner * 6 + n]
            value = parts[0, index].astype(jnp.float32) + parts[1, index].astype(jnp.float32)
            slots[owner, n] = (value * slot_used[owner * 6 + n].astype(jnp.float32)).astype(jnp.bfloat16)
            return inner

        lax.fori_loop(0, 6, one, 0)

    def slot_copy(owner, index, device):
        return remote(slots.at[owner], out_ref.at[c], o_send.at[index], o_recv.at[index], device)

    for index, (owner, device) in enumerate(((z2, to_z2), (zp, to_zp), (zm, to_zm))):
        fill(owner)
        slot_copy(owner, index, device).start()
    fill(c)
    stay = pltpu.make_async_copy(slots.at[c], out_ref.at[c], local_sem.at[5])
    stay.start()
    for phase in range(2):
        ref = abuf.at[phase, pl.ds(0, 15)]
        remote(ref, ref, a_send.at[phase], core_recv.at[phase, 0], to_b).wait_send()
    keep_copy.wait_send()
    b_full_over_y().wait_send()
    edges_over_y(r, lambda copy: copy.wait_send())

    def all_sent(part, inner):
        b_sent(part)
        return inner

    lax.fori_loop(0, 5, all_sent, 0)
    column_copy(0, to_other_column).wait_send()

    @pl.when(y != l)
    def _():
        column_copy(1, to_l).wait_send()

    middle_copy().wait_send()
    stay.wait()
    for index, (owner, device, sender) in enumerate(((z2, to_z2, z2), (zp, to_zp, zm), (zm, to_zm, zp))):
        slot_copy(owner, index, device).wait_send()
        remote(slots.at[owner], out_ref.at[sender], o_send.at[index], o_recv.at[index], device).wait_recv()


def on_device(a_blocks, b_blocks, a_offsets, b_offsets, keep_offsets, owners):
    a_part = a_blocks.reshape(12, BLOCK, BLOCK)
    b_part = b_blocks.reshape(4, 8, BLOCK, BLOCK)
    keep = keep_offsets[:, 0, 0]
    smem = pl.BlockSpec(memory_space=pltpu.SMEM)
    anywhere = pl.BlockSpec(memory_space=pl.ANY)
    dma = pltpu.SemaphoreType.DMA
    block = (BLOCK, BLOCK)
    arrived = pl.pallas_call(
        kernel,
        out_shape=jax.ShapeDtypeStruct((4, 6, BLOCK, BLOCK), jnp.bfloat16),
        in_specs=[anywhere, anywhere, smem, smem, smem, smem, pl.BlockSpec(memory_space=pltpu.VMEM)],
        out_specs=anywhere,
        scratch_shapes=[
            pltpu.VMEM((2, 16, 4) + block, jnp.bfloat16),
            pltpu.VMEM((5, 4, 4) + block, jnp.bfloat16),
            pltpu.VMEM((8,) + block, jnp.float32),
            pltpu.VMEM((2, 12) + block, jnp.bfloat16),
            pltpu.VMEM((2, 8) + block, jnp.bfloat16),
            pltpu.VMEM((4,) + block, jnp.bfloat16),
            pltpu.VMEM((4, 6) + block, jnp.bfloat16),
            pltpu.VMEM((1, 24), jnp.int32),
            pltpu.SMEM((1, 24), jnp.int32),
            pltpu.SMEM((24,), jnp.int32),
            pltpu.SMEM((256,), jnp.int32),
            pltpu.SMEM((12,), jnp.int32),
            pltpu.SMEM((24,), jnp.int32),
            pltpu.SMEM((24,), jnp.int32),
            dma((7,)),
            dma((2,)),
            dma((2,)),
            dma((2,)),
            dma((2, 2, 2)),
            dma((2, 2, 2)),
            dma((2, 8)),
            dma((5,)),
            dma((5,)),
            dma((3, 5, 4)),
            dma((3, 5, 4)),
            dma((3,)),
            dma((3,)),
            dma((3,)),
            dma((3,)),
        ],
        compiler_params=pltpu.CompilerParams(
            collective_id=0, has_side_effects=True, vmem_limit_bytes=56 << 20
        ),
        cost_estimate=pl.CostEstimate(
            flops=192 * 2 * BLOCK**3, bytes_accessed=10 << 20, transcendentals=0
        ),
        name="banded_product",
    )(
        a_part,
        b_part,
        a_offsets[:, 0, :].T,
        b_offsets.T,
        keep,
        owners[:, 0, 0],
        keep.reshape(1, 24),
    )
    return arrived.reshape(1, 1, 1, 4, 6, BLOCK, BLOCK)


def solution(mesh):
    return jax.shard_map(
        on_device,
        mesh=mesh,
        in_specs=(
            P("row", "col", "layer", None, None, None),
            P("row", "col", "layer", None, None, None),
            P(None, "col", None),
            P(),
            P(None, "col", "row"),
            P("layer", "col", "row"),
        ),
        out_specs=P("row", "col", "layer", None, None, None, None),
        check_vma=False,
    )
```

```python
import functools

import jax
import jax.numpy as jnp
from jax import lax
from jax.experimental import pallas as pl
from jax.experimental.pallas import tpu as pltpu
from jax.sharding import PartitionSpec as P

MESH = pl.DeviceIdType.MESH
BLOCK = 256


def mod(value, count):
    return lax.rem(value + 32 * count, jnp.int32(count))


def kernel(
    a_ref,
    b_ref,
    a_offsets,
    b_offsets,
    keep,
    owners,
    keep_vector,
    out_ref,
    abuf,
    bbuf,
    total,
    parts,
    leaving,
    swapped,
    slots,
    keep_arrived,
    keep_other,
    a_mask,
    b_mask,
    rank,
    slot_source,
    slot_used,
    local_sem,
    keep_sem,
    a_send,
    yy_recv,
    yx_recv,
    yx2_recv,
    core_recv,
    by_send,
    by_recv,
    bz_send,
    bz_recv,
    p_send,
    p_recv,
    o_send,
    o_recv,
):
    r = lax.axis_index("row")
    c = lax.axis_index("col")
    l = lax.axis_index("layer")
    x, y, b = r // 4, (r // 2) % 2, r % 2

    def row_of(xx, yy, bb):
        return xx * 4 + yy * 2 + bb

    xp, xm, x2 = mod(x + 1, 4), mod(x - 1, 4), mod(x + 2, 4)
    zp, zm, z2 = mod(c + 1, 4), mod(c - 1, 4), mod(c + 2, 4)
    y1, b1, l1 = 1 - y, 1 - b, 1 - l
    r1 = row_of(x, y1, b)
    to_xp, to_xm = {"row": row_of(xp, y, b)}, {"row": row_of(xm, y, b)}
    to_y, to_b = {"row": r1}, {"row": row_of(x, y, b1)}
    to_zp, to_zm, to_z2 = {"col": zp}, {"col": zm}, {"col": z2}
    to_l, to_yl = {"layer": l1}, {"row": r1, "layer": l1}

    barrier = pltpu.get_barrier_semaphore()
    for device in (to_xp, to_xm, to_y, to_b, to_zp, to_zm, to_z2, to_l, to_yl):
        pl.semaphore_signal(barrier, inc=1, device_id=device, device_id_type=MESH)
    pl.semaphore_wait(barrier, 9)

    def remote(src, dst, send, recv, device):
        return pltpu.make_async_remote_copy(
            src_ref=src, dst_ref=dst, send_sem=send, recv_sem=recv, device_id=device, device_id_type=MESH
        )

    def third(phase):
        return 2 * y if phase == 0 else 1

    def pass_a(source, phase, first, count, recv, device):
        ref = abuf.at[phase, source, pl.ds(first, count)]
        remote(ref, ref, a_send.at[phase], recv, device).start()

    def got_a(source, phase, first, count, recv):
        ref = abuf.at[phase, source, pl.ds(first, count)]
        remote(ref, ref, a_send.at[phase], recv, to_b).wait_recv()

    def own_copy(phase):
        return pltpu.make_async_copy(
            a_ref.at[pl.ds(third(phase) * 4, 4)], abuf.at[phase, r], local_sem.at[phase]
        )

    def a_to_y(phase):
        first = 8 * y1 if phase == 0 else 4
        remote(
            a_ref.at[pl.ds(first, 4)], abuf.at[phase, r], a_send.at[phase], yy_recv.at[phase], to_y
        ).start()

    def a_along_x(phase, yy):
        index = 0 if yy is y else 1
        s = row_of(x, yy, b)
        pass_a(s, phase, 0, 4, yx_recv.at[phase, index, 0], to_xp)
        pass_a(s, phase, 0, 4, yx_recv.at[phase, index, 1], to_xm)

    def a_further(phase, yy):
        index = 0 if yy is y else 1
        s = row_of(xm, yy, b)
        got_a(s, phase, 0, 4, yx_recv.at[phase, index, 0])
        pass_a(s, phase, 0, 2, yx2_recv.at[phase, index, 0], to_xp)
        s = row_of(xp, yy, b)
        got_a(s, phase, 0, 4, yx_recv.at[phase, index, 1])
        pass_a(s, phase, 2, 2, yx2_recv.at[phase, index, 1], to_xm)

    def to_sibling(phase, n):
        source = row_of(mod(x + n, 4), mod(y + n // 4, 2), b)
        pass_a(source, phase, 0, 4, core_recv.at[phase, n], to_b)

    def a_last(phase, yy):
        index = 0 if yy is y else 1
        s = row_of(x2, yy, b)
        got_a(s, phase, 0, 2, yx2_recv.at[phase, index, 0])
        got_a(s, phase, 2, 2, yx2_recv.at[phase, index, 1])

    other_full, other_edge = 3 + l, 4 - l
    own_second, own_last = 2 * y, 2 - 2 * y

    def b_own_copy(part):
        return pltpu.make_async_copy(
            b_ref.at[:, mod(y + part - l, 8)], bbuf.at[part, c], local_sem.at[2 + part]
        )

    def b_full_over_y():
        return remote(
            b_ref.at[:, mod(2 * y1, 8)], bbuf.at[other_full, c], by_send.at[4], by_recv.at[4], to_y
        )

    def b_edge_over_y(n):
        return remote(
            b_ref.at[n, mod(2 * y1 + 1 - 2 * l, 8)],
            bbuf.at[other_edge, c, n],
            by_send.at[n],
            by_recv.at[n],
            to_y,
        )

    def near(column, source, n):
        q = mod(column + 4 * source + n, 16)
        return jnp.where(l == 0, jnp.where(q <= 6, 1, 0), jnp.where(q >= 8, 1, 0))

    def edges_over_y(column, act):
        for n in range(4):

            @pl.when(near(column, c, n) == 1)
            def _():
                act(b_edge_over_y(n))

    def inside(part, source, n):
        column = jnp.where(part >= 3, r1, r)
        whole = jnp.where(part >= 3, jnp.where(part == other_full, 1, 0), jnp.where(part == 2 * l1, 0, 1))
        return whole + near(column, source, n) > 0

    def b_copy(part, source, n, way, device):
        ref = bbuf.at[part, source, n]
        return remote(ref, ref, bz_send.at[way, part, n], bz_recv.at[way, part, n], device)

    def b_start(part):
        for n in range(4):

            @pl.when(inside(part, c, n))
            def _():
                b_copy(part, c, n, 0, to_zp).start()
                b_copy(part, c, n, 1, to_zm).start()

    def b_further(part):
        for n in range(4):

            @pl.when(inside(part, zm, n))
            def _():
                b_copy(part, zm, n, 0, to_zp).wait_recv()
                if n < 2:
                    b_copy(part, zm, n, 2, to_zp).start()

            @pl.when(inside(part, zp, n))
            def _():
                b_copy(part, zp, n, 1, to_zm).wait_recv()
                if n >= 2:
                    b_copy(part, zp, n, 2, to_zm).start()

    def b_last(part):
        for n in range(4):

            @pl.when(inside(part, z2, n))
            def _():
                b_copy(part, z2, n, 2, to_zp).wait_recv()

    def b_sent(part):
        for n in range(4):

            @pl.when(inside(part, c, n))
            def _():
                b_copy(part, c, n, 0, to_zp).wait_send()
                b_copy(part, c, n, 1, to_zm).wait_send()

            @pl.when(inside(part, zm if n < 2 else zp, n))
            def _():
                b_copy(part, c, n, 2, to_zp).wait_send()

    def multiply(source, phase, column, keeps, first_part):
        piece = 16 * l + mod(source + 4 * c, 16)
        top = mod(piece - c + 8, 32) // 4
        for g in range(4):
            u = jnp.where(top >= 3, top - 3 + g, jnp.where(g <= top, g, g + 4))
            t = 8 * third(phase) + u
            i = c + 4 * t
            d = mod(piece - i + 8, 32) - 8
            k = mod(i + d, 256)
            part = mod(k // 32 + l, 8) + first_part
            e = mod(column - k + 8, 16) - 8
            distance = mod(k - column, 16)
            present = (
                lax.shift_right_logical(a_mask[t], d + 8) & lax.shift_right_logical(b_mask[k], e + 8) & 1
            )
            weight = jnp.where(keeps(t) == d + e, present, 0).astype(jnp.float32)
            product = jnp.dot(
                abuf[phase, source, g],
                bbuf[part, distance // 4, distance % 4],
                preferred_element_type=jnp.float32,
            )
            total[u] += product * weight

    def own_keep(t):
        return keep[t]

    def other_keep(t):
        return keep_other[0, t]

    def add_sources(phase, column, keeps, first_part, wait):
        total[...] = jnp.zeros_like(total)

        def of_this_core(n, inner):
            multiply(row_of(mod(x + n, 4), mod(y + n // 4, 2), b), phase, column, keeps, first_part)
            return inner

        lax.fori_loop(0, 8, of_this_core, 0)

        def of_sibling(n, inner):
            source = row_of(mod(x + n, 4), mod(y + n // 4, 2), b1)
            if wait:
                got_a(source, phase, 0, 4, core_recv.at[phase, n])
            multiply(source, phase, column, keeps, first_part)
            return inner

        lax.fori_loop(0, 8, of_sibling, 0)

    def add_middle(first, count):
        def place(at):
            early = at + jnp.where(at >= 2, 1, 0) + jnp.where(at >= 5, 1, 0)
            return jnp.where(at < 6, early, 4 * at - 22)

        def of_this_core(at, inner):
            n = place(at)
            source = row_of(mod(x + n, 4), mod(y + n // 4, 2), b)
            multiply(source, 1, r, own_keep, -y)
            return inner

        def of_sibling(at, inner):
            n = place(at)
            source = row_of(mod(x + n, 4), mod(y + n // 4, 2), b1)
            got_a(source, 1, 0, 4, core_recv.at[1, n])
            multiply(source, 1, r, own_keep, -y)
            return inner

        lax.fori_loop(first, first + count, of_this_core, 0)
        lax.fori_loop(first, first + count, of_sibling, 0)

    def store_rows(put, count, row):
        def one(n, inner):
            put(n, total[row + n].astype(jnp.bfloat16))
            return inner

        lax.fori_loop(0, count, one, 0)

    def column_copy(index, device):
        return remote(
            leaving.at[index],
            parts.at[l, pl.ds(4 * y, 8)],
            p_send.at[index],
            p_recv.at[l],
            device,
        )

    to_other_column = {"row": r1, "layer": y}

    def middle_copy():
        return remote(swapped, parts.at[l, pl.ds(8 * l, 4)], p_send.at[2], p_recv.at[2], to_l)

    def bits(offsets, at):
        found = jnp.int32(0)
        for n in range(12):
            found += lax.shift_left(jnp.int32(1), offsets(n, at) + 8)
        return found

    def plan():
        def a_row(t, inner):
            a_mask[t] = bits(lambda n, at: a_offsets[n, 0, at], t)
            return inner

        lax.fori_loop(0, 24, a_row, 0)

        def b_row(n, inner):
            k = mod(n - 8, 256)
            b_mask[k] = bits(lambda n, at: b_offsets[n, at], k)
            return inner

        lax.fori_loop(0, 111, b_row, 0)
        for t in range(12):
            before = jnp.int32(0)
            for n in range(t):
                before += jnp.where(owners[n] == owners[t], 1, 0)
            rank[t] = before

        def slot(at, inner):
            owner, place = at // 6, at % 6
            source, used = jnp.int32(0), jnp.int32(0)
            for t in range(12):
                here = jnp.where((owners[t] == owner) & (rank[t] == place), 1, 0)
                source += here * t
                used += here
            slot_source[at] = source
            slot_used[at] = used
            return inner

        lax.fori_loop(0, 24, slot, 0)

    own_copy(0).start()
    b_own_copy(1).start()
    b_own_copy(own_second).start()
    own_copy(1).start()
    b_own_copy(own_last).start()
    a_to_y(0)
    b_full_over_y().start()
    keep_copy = remote(keep_vector, keep_arrived, keep_sem.at[0], keep_sem.at[1], to_y)
    keep_copy.start()
    own_copy(0).wait()
    a_along_x(0, y)
    b_own_copy(1).wait()
    b_start(1)
    b_own_copy(own_second).wait()
    b_start(own_second)
    to_sibling(0, 0)
    plan()
    got_a(r1, 0, 0, 4, yy_recv.at[0])
    a_along_x(0, y1)
    own_copy(1).wait()
    a_along_x(1, y)
    edges_over_y(r, lambda copy: copy.start())
    b_full_over_y().wait_recv()
    b_start(other_full)
    a_to_y(1)
    to_sibling(0, 4)
    a_further(0, y)
    b_further(1)
    to_sibling(0, 1)
    to_sibling(0, 3)
    b_further(own_second)
    edges_over_y(r1, lambda copy: copy.wait_recv())
    b_start(other_edge)
    a_further(0, y1)
    to_sibling(0, 5)
    to_sibling(0, 7)
    got_a(r1, 1, 0, 4, yy_recv.at[1])
    a_along_x(1, y1)
    b_further(other_full)
    b_own_copy(own_last).wait()
    b_start(own_last)
    a_further(1, y)
    a_last(0, y)
    to_sibling(0, 2)
    a_last(0, y1)
    to_sibling(0, 6)
    to_sibling(1, 0)
    to_sibling(1, 4)
    b_last(1)
    b_last(own_second)
    b_further(other_edge)
    add_sources(0, r, own_keep, -y, True)

    @pl.when(y == l)
    def _():
        def put_here(n, value):
            parts[l, 4 * y + n] = value

        store_rows(put_here, 8, 0)

    @pl.when(y != l)
    def _():
        def put_own(n, value):
            leaving[1, n] = value

        store_rows(put_own, 8, 0)
        column_copy(1, to_l).start()

    to_sibling(1, 1)
    to_sibling(1, 3)
    a_further(1, y1)
    to_sibling(1, 5)
    to_sibling(1, 7)
    keep_copy.wait_recv()
    keep_local = pltpu.make_async_copy(keep_arrived, keep_other, local_sem.at[6])
    keep_local.start()
    keep_local.wait()
    b_last(other_full)
    b_last(other_edge)
    add_sources(0, r1, other_keep, 3 - 2 * y, False)

    def put_other(n, value):
        leaving[0, n] = value

    store_rows(put_other, 8, 0)
    column_copy(0, to_other_column).start()
    b_further(own_last)

    b_last(own_last)
    total[...] = jnp.zeros_like(total)
    add_middle(0, 6)
    a_last(1, y)
    to_sibling(1, 2)
    a_last(1, y1)
    to_sibling(1, 6)
    add_middle(6, 2)

    def put_middle(n, value):
        swapped[n] = value

    store_rows(put_middle, 4, 4 * l1)
    middle_copy().start()

    def put_middle_here(n, value):
        parts[l, 8 * l1 + n] = value

    store_rows(put_middle_here, 4, 4 * l)

    def part_arrived(layer):
        ref = parts.at[layer, pl.ds(4 * l, 8)]
        remote(leaving.at[0], ref, p_send.at[0], p_recv.at[layer], to_l).wait_recv()

    @pl.when(y == l)
    def _():
        part_arrived(l1)

    @pl.when(y != l)
    def _():
        part_arrived(0)
        part_arrived(1)

    remote(swapped, parts.at[l1, pl.ds(8 * l1, 4)], p_send.at[2], p_recv.at[2], to_l).wait_recv()

    def fill(owner):
        def one(n, inner):
            index = slot_source[owner * 6 + n]
            value = parts[0, index].astype(jnp.float32) + parts[1, index].astype(jnp.float32)
            slots[owner, n] = (value * slot_used[owner * 6 + n].astype(jnp.float32)).astype(jnp.bfloat16)
            return inner

        lax.fori_loop(0, 6, one, 0)

    def slot_copy(owner, index, device):
        return remote(slots.at[owner], out_ref.at[c], o_send.at[index], o_recv.at[index], device)

    for index, (owner, device) in enumerate(((z2, to_z2), (zp, to_zp), (zm, to_zm))):
        fill(owner)
        slot_copy(owner, index, device).start()
    fill(c)
    stay = pltpu.make_async_copy(slots.at[c], out_ref.at[c], local_sem.at[5])
    stay.start()
    for phase in range(2):
        ref = abuf.at[phase, pl.ds(0, 15)]
        remote(ref, ref, a_send.at[phase], core_recv.at[phase, 0], to_b).wait_send()
    keep_copy.wait_send()
    b_full_over_y().wait_send()
    edges_over_y(r, lambda copy: copy.wait_send())

    def all_sent(part, inner):
        b_sent(part)
        return inner

    lax.fori_loop(0, 5, all_sent, 0)
    column_copy(0, to_other_column).wait_send()

    @pl.when(y != l)
    def _():
        column_copy(1, to_l).wait_send()

    middle_copy().wait_send()
    stay.wait()
    for index, (owner, device, sender) in enumerate(((z2, to_z2, z2), (zp, to_zp, zm), (zm, to_zm, zp))):
        slot_copy(owner, index, device).wait_send()
        remote(slots.at[owner], out_ref.at[sender], o_send.at[index], o_recv.at[index], device).wait_recv()


def on_device(a_blocks, b_blocks, a_offsets, b_offsets, keep_offsets, owners):
    a_part = a_blocks.reshape(12, BLOCK, BLOCK)
    b_part = b_blocks.reshape(4, 8, BLOCK, BLOCK)
    keep = keep_offsets[:, 0, 0]
    smem = pl.BlockSpec(memory_space=pltpu.SMEM)
    anywhere = pl.BlockSpec(memory_space=pl.ANY)
    dma = pltpu.SemaphoreType.DMA
    block = (BLOCK, BLOCK)
    arrived = pl.pallas_call(
        kernel,
        out_shape=jax.ShapeDtypeStruct((4, 6, BLOCK, BLOCK), jnp.bfloat16),
        in_specs=[anywhere, anywhere, smem, smem, smem, smem, pl.BlockSpec(memory_space=pltpu.VMEM)],
        out_specs=anywhere,
        scratch_shapes=[
            pltpu.VMEM((2, 16, 4) + block, jnp.bfloat16),
            pltpu.VMEM((5, 4, 4) + block, jnp.bfloat16),
            pltpu.VMEM((8,) + block, jnp.float32),
            pltpu.VMEM((2, 12) + block, jnp.bfloat16),
            pltpu.VMEM((2, 8) + block, jnp.bfloat16),
            pltpu.VMEM((4,) + block, jnp.bfloat16),
            pltpu.VMEM((4, 6) + block, jnp.bfloat16),
            pltpu.VMEM((1, 24), jnp.int32),
            pltpu.SMEM((1, 24), jnp.int32),
            pltpu.SMEM((24,), jnp.int32),
            pltpu.SMEM((256,), jnp.int32),
            pltpu.SMEM((12,), jnp.int32),
            pltpu.SMEM((24,), jnp.int32),
            pltpu.SMEM((24,), jnp.int32),
            dma((7,)),
            dma((2,)),
            dma((2,)),
            dma((2,)),
            dma((2, 2, 2)),
            dma((2, 2, 2)),
            dma((2, 8)),
            dma((5,)),
            dma((5,)),
            dma((3, 5, 4)),
            dma((3, 5, 4)),
            dma((3,)),
            dma((3,)),
            dma((3,)),
            dma((3,)),
        ],
        compiler_params=pltpu.CompilerParams(
            collective_id=0, has_side_effects=True, vmem_limit_bytes=56 << 20
        ),
        cost_estimate=pl.CostEstimate(
            flops=192 * 2 * BLOCK**3, bytes_accessed=10 << 20, transcendentals=0
        ),
        name="banded_product",
    )(
        a_part,
        b_part,
        a_offsets.transpose(2, 1, 0),
        b_offsets.T,
        keep,
        owners[:, 0, 0],
        keep.reshape(1, 24),
    )
    return arrived.reshape(1, 1, 1, 4, 6, BLOCK, BLOCK)


def solution(mesh):
    return jax.shard_map(
        on_device,
        mesh=mesh,
        in_specs=(
            P("row", "col", "layer", None, None, None),
            P("row", "col", "layer", None, None, None),
            P(None, "col", None),
            P(),
            P(None, "col", "row"),
            P("layer", "col", "row"),
        ),
        out_specs=P("row", "col", "layer", None, None, None, None),
        check_vma=False,
    )
```

```python
import functools

import jax
import jax.numpy as jnp
from jax import lax
from jax.experimental import pallas as pl
from jax.experimental.pallas import tpu as pltpu
from jax.sharding import PartitionSpec as P

MESH = pl.DeviceIdType.MESH
BLOCK = 256


def mod(value, count):
    return lax.rem(value + 32 * count, jnp.int32(count))


def kernel(
    a_ref,
    b_ref,
    a_offsets,
    b_offsets,
    keep,
    owners,
    keep_vector,
    out_ref,
    abuf,
    bbuf,
    total,
    parts,
    leaving,
    swapped,
    slots,
    keep_arrived,
    keep_other,
    a_mask,
    b_mask,
    rank,
    slot_source,
    slot_used,
    local_sem,
    keep_sem,
    a_send,
    yy_recv,
    yx_recv,
    yx2_recv,
    core_recv,
    by_send,
    by_recv,
    bz_send,
    bz_recv,
    p_send,
    p_recv,
    o_send,
    o_recv,
):
    r = lax.axis_index("row")
    c = lax.axis_index("col")
    l = lax.axis_index("layer")
    x, y, b = r // 4, (r // 2) % 2, r % 2

    def row_of(xx, yy, bb):
        return xx * 4 + yy * 2 + bb

    xp, xm, x2 = mod(x + 1, 4), mod(x - 1, 4), mod(x + 2, 4)
    zp, zm, z2 = mod(c + 1, 4), mod(c - 1, 4), mod(c + 2, 4)
    y1, b1, l1 = 1 - y, 1 - b, 1 - l
    r1 = row_of(x, y1, b)
    to_xp, to_xm = {"row": row_of(xp, y, b)}, {"row": row_of(xm, y, b)}
    to_y, to_b = {"row": r1}, {"row": row_of(x, y, b1)}
    to_zp, to_zm, to_z2 = {"col": zp}, {"col": zm}, {"col": z2}
    to_l, to_yl = {"layer": l1}, {"row": r1, "layer": l1}

    barrier = pltpu.get_barrier_semaphore()
    for device in (to_xp, to_xm, to_y, to_b, to_zp, to_zm, to_z2, to_l, to_yl):
        pl.semaphore_signal(barrier, inc=1, device_id=device, device_id_type=MESH)
    pl.semaphore_wait(barrier, 9)

    def remote(src, dst, send, recv, device):
        return pltpu.make_async_remote_copy(
            src_ref=src, dst_ref=dst, send_sem=send, recv_sem=recv, device_id=device, device_id_type=MESH
        )

    def third(phase):
        return 2 * y if phase == 0 else 1

    def pass_a(source, phase, first, count, recv, device):
        ref = abuf.at[phase, source, pl.ds(first, count)]
        remote(ref, ref, a_send.at[phase], recv, device).start()

    def got_a(source, phase, first, count, recv):
        ref = abuf.at[phase, source, pl.ds(first, count)]
        remote(ref, ref, a_send.at[phase], recv, to_b).wait_recv()

    def own_copy(phase):
        return pltpu.make_async_copy(
            a_ref.at[pl.ds(third(phase) * 4, 4)], abuf.at[phase, r], local_sem.at[phase]
        )

    def a_to_y(phase):
        first = 8 * y1 if phase == 0 else 4
        remote(
            a_ref.at[pl.ds(first, 4)], abuf.at[phase, r], a_send.at[phase], yy_recv.at[phase], to_y
        ).start()

    def a_along_x(phase, yy):
        index = 0 if yy is y else 1
        s = row_of(x, yy, b)
        pass_a(s, phase, 0, 4, yx_recv.at[phase, index, 0], to_xp)
        pass_a(s, phase, 0, 4, yx_recv.at[phase, index, 1], to_xm)

    def a_further(phase, yy):
        index = 0 if yy is y else 1
        s = row_of(xm, yy, b)
        got_a(s, phase, 0, 4, yx_recv.at[phase, index, 0])
        pass_a(s, phase, 0, 2, yx2_recv.at[phase, index, 0], to_xp)
        s = row_of(xp, yy, b)
        got_a(s, phase, 0, 4, yx_recv.at[phase, index, 1])
        pass_a(s, phase, 2, 2, yx2_recv.at[phase, index, 1], to_xm)

    def to_sibling(phase, n):
        source = row_of(mod(x + n, 4), mod(y + n // 4, 2), b)
        pass_a(source, phase, 0, 4, core_recv.at[phase, n], to_b)

    def a_last(phase, yy):
        index = 0 if yy is y else 1
        s = row_of(x2, yy, b)
        got_a(s, phase, 0, 2, yx2_recv.at[phase, index, 0])
        got_a(s, phase, 2, 2, yx2_recv.at[phase, index, 1])

    other_full, other_edge = 3 + l, 4 - l
    own_second, own_last = 2 * y, 2 - 2 * y

    def b_own_copy(part):
        return pltpu.make_async_copy(
            b_ref.at[:, mod(y + part - l, 8)], bbuf.at[part, c], local_sem.at[2 + part]
        )

    def b_full_over_y():
        return remote(
            b_ref.at[:, mod(2 * y1, 8)], bbuf.at[other_full, c], by_send.at[4], by_recv.at[4], to_y
        )

    def b_edge_over_y(n):
        return remote(
            b_ref.at[n, mod(2 * y1 + 1 - 2 * l, 8)],
            bbuf.at[other_edge, c, n],
            by_send.at[n],
            by_recv.at[n],
            to_y,
        )

    def near(column, source, n):
        q = mod(column + 4 * source + n, 16)
        return jnp.where(l == 0, jnp.where(q <= 6, 1, 0), jnp.where(q >= 8, 1, 0))

    def edges_over_y(column, act):
        for n in range(4):

            @pl.when(near(column, c, n) == 1)
            def _():
                act(b_edge_over_y(n))

    def inside(part, source, n):
        column = jnp.where(part >= 3, r1, r)
        whole = jnp.where(part >= 3, jnp.where(part == other_full, 1, 0), jnp.where(part == 2 * l1, 0, 1))
        return whole + near(column, source, n) > 0

    def b_copy(part, source, n, way, device):
        ref = bbuf.at[part, source, n]
        return remote(ref, ref, bz_send.at[way, part, n], bz_recv.at[way, part, n], device)

    def b_start(part):
        for n in range(4):

            @pl.when(inside(part, c, n))
            def _():
                b_copy(part, c, n, 0, to_zp).start()
                b_copy(part, c, n, 1, to_zm).start()

    def b_further(part):
        for n in range(4):

            @pl.when(inside(part, zm, n))
            def _():
                b_copy(part, zm, n, 0, to_zp).wait_recv()
                if n < 2:
                    b_copy(part, zm, n, 2, to_zp).start()

            @pl.when(inside(part, zp, n))
            def _():
                b_copy(part, zp, n, 1, to_zm).wait_recv()
                if n >= 2:
                    b_copy(part, zp, n, 2, to_zm).start()

    def b_last(part):
        for n in range(4):

            @pl.when(inside(part, z2, n))
            def _():
                b_copy(part, z2, n, 2, to_zp).wait_recv()

    def b_sent(part):
        for n in range(4):

            @pl.when(inside(part, c, n))
            def _():
                b_copy(part, c, n, 0, to_zp).wait_send()
                b_copy(part, c, n, 1, to_zm).wait_send()

            @pl.when(inside(part, zm if n < 2 else zp, n))
            def _():
                b_copy(part, c, n, 2, to_zp).wait_send()

    def multiply(source, phase, column, keeps, first_part):
        piece = 16 * l + mod(source + 4 * c, 16)
        top = mod(piece - c + 8, 32) // 4
        for g in range(4):
            u = jnp.where(top >= 3, top - 3 + g, jnp.where(g <= top, g, g + 4))
            t = 8 * third(phase) + u
            i = c + 4 * t
            d = mod(piece - i + 8, 32) - 8
            k = mod(i + d, 256)
            part = mod(k // 32 + l, 8) + first_part
            e = mod(column - k + 8, 16) - 8
            distance = mod(k - column, 16)
            present = (
                lax.shift_right_logical(a_mask[t], d + 8) & lax.shift_right_logical(b_mask[k], e + 8) & 1
            )
            weight = jnp.where(keeps(t) == d + e, present, 0).astype(jnp.float32)
            product = jnp.dot(
                abuf[phase, source, g],
                bbuf[part, distance // 4, distance % 4],
                preferred_element_type=jnp.float32,
            )
            total[u] += product * weight

    def own_keep(t):
        return keep[t]

    def other_keep(t):
        return keep_other[0, t]

    def add_sources(phase, column, keeps, first_part, wait):
        total[...] = jnp.zeros_like(total)

        def of_this_core(n, inner):
            multiply(row_of(mod(x + n, 4), mod(y + n // 4, 2), b), phase, column, keeps, first_part)
            return inner

        lax.fori_loop(0, 8, of_this_core, 0)

        def of_sibling(n, inner):
            source = row_of(mod(x + n, 4), mod(y + n // 4, 2), b1)
            if wait:
                got_a(source, phase, 0, 4, core_recv.at[phase, n])
            multiply(source, phase, column, keeps, first_part)
            return inner

        lax.fori_loop(0, 8, of_sibling, 0)

    def add_middle(first, count):
        def place(at):
            early = at + jnp.where(at >= 2, 1, 0) + jnp.where(at >= 5, 1, 0)
            return jnp.where(at < 6, early, 4 * at - 22)

        def of_this_core(at, inner):
            n = place(at)
            source = row_of(mod(x + n, 4), mod(y + n // 4, 2), b)
            multiply(source, 1, r, own_keep, -y)
            return inner

        def of_sibling(at, inner):
            n = place(at)
            source = row_of(mod(x + n, 4), mod(y + n // 4, 2), b1)
            got_a(source, 1, 0, 4, core_recv.at[1, n])
            multiply(source, 1, r, own_keep, -y)
            return inner

        lax.fori_loop(first, first + count, of_this_core, 0)
        lax.fori_loop(first, first + count, of_sibling, 0)

    def store_rows(put, count, row):
        def one(n, inner):
            put(n, total[row + n].astype(jnp.bfloat16))
            return inner

        lax.fori_loop(0, count, one, 0)

    def column_copy(index, device):
        return remote(
            leaving.at[index],
            parts.at[l, pl.ds(4 * y, 8)],
            p_send.at[index],
            p_recv.at[l],
            device,
        )

    to_other_column = {"row": r1, "layer": y}

    def middle_copy():
        return remote(swapped, parts.at[l, pl.ds(8 * l, 4)], p_send.at[2], p_recv.at[2], to_l)

    def bits(offsets, at):
        found = jnp.int32(0)
        for n in range(12):
            found += lax.shift_left(jnp.int32(1), offsets(n, at) + 8)
        return found

    def plan():
        def a_row(t, inner):
            a_mask[t] = bits(lambda n, at: a_offsets[n, 0, at], t)
            return inner

        lax.fori_loop(0, 24, a_row, 0)

        def b_row(n, inner):
            k = mod(n - 8, 256)
            b_mask[k] = bits(lambda n, at: b_offsets[n, at], k)
            return inner

        lax.fori_loop(0, 111, b_row, 0)
        for t in range(12):
            before = jnp.int32(0)
            for n in range(t):
                before += jnp.where(owners[n] == owners[t], 1, 0)
            rank[t] = before

        def slot(at, inner):
            owner, place = at // 6, at % 6
            source, used = jnp.int32(0), jnp.int32(0)
            for t in range(12):
                here = jnp.where((owners[t] == owner) & (rank[t] == place), 1, 0)
                source += here * t
                used += here
            slot_source[at] = source
            slot_used[at] = used
            return inner

        lax.fori_loop(0, 24, slot, 0)

    own_copy(0).start()
    b_own_copy(1).start()
    b_own_copy(own_second).start()
    own_copy(1).start()
    b_own_copy(own_last).start()
    a_to_y(0)
    b_full_over_y().start()
    keep_copy = remote(keep_vector, keep_arrived, keep_sem.at[0], keep_sem.at[1], to_y)
    keep_copy.start()
    own_copy(0).wait()
    a_along_x(0, y)
    b_own_copy(1).wait()
    b_start(1)
    b_own_copy(own_second).wait()
    b_start(own_second)
    to_sibling(0, 0)
    plan()
    got_a(r1, 0, 0, 4, yy_recv.at[0])
    a_along_x(0, y1)
    own_copy(1).wait()
    a_along_x(1, y)
    edges_over_y(r, lambda copy: copy.start())
    b_full_over_y().wait_recv()
    b_start(other_full)
    a_to_y(1)
    to_sibling(0, 4)
    a_further(0, y)
    b_further(1)
    to_sibling(0, 1)
    to_sibling(0, 3)
    b_further(own_second)
    edges_over_y(r1, lambda copy: copy.wait_recv())
    b_start(other_edge)
    a_further(0, y1)
    to_sibling(0, 5)
    to_sibling(0, 7)
    got_a(r1, 1, 0, 4, yy_recv.at[1])
    a_along_x(1, y1)
    b_further(other_full)
    b_own_copy(own_last).wait()
    b_start(own_last)
    a_further(1, y)
    a_last(0, y)
    to_sibling(0, 2)
    a_last(0, y1)
    to_sibling(0, 6)
    to_sibling(1, 0)
    to_sibling(1, 4)
    b_last(1)
    b_last(own_second)
    b_further(other_edge)
    add_sources(0, r, own_keep, -y, True)

    @pl.when(y == l)
    def _():
        def put_here(n, value):
            parts[l, 4 * y + n] = value

        store_rows(put_here, 8, 0)

    @pl.when(y != l)
    def _():
        def put_own(n, value):
            leaving[1, n] = value

        store_rows(put_own, 8, 0)
        column_copy(1, to_l).start()

    to_sibling(1, 1)
    to_sibling(1, 3)
    a_further(1, y1)
    to_sibling(1, 5)
    to_sibling(1, 7)
    keep_copy.wait_recv()
    keep_local = pltpu.make_async_copy(keep_arrived, keep_other, local_sem.at[6])
    keep_local.start()
    keep_local.wait()
    b_last(other_full)
    b_last(other_edge)
    add_sources(0, r1, other_keep, 3 - 2 * y, False)

    def put_other(n, value):
        leaving[0, n] = value

    store_rows(put_other, 8, 0)
    column_copy(0, to_other_column).start()
    b_further(own_last)

    b_last(own_last)
    total[...] = jnp.zeros_like(total)
    add_middle(0, 6)
    a_last(1, y)
    to_sibling(1, 2)
    a_last(1, y1)
    to_sibling(1, 6)
    add_middle(6, 2)

    def put_middle(n, value):
        swapped[n] = value

    store_rows(put_middle, 4, 4 * l1)
    middle_copy().start()

    def put_middle_here(n, value):
        parts[l, 8 * l1 + n] = value

    store_rows(put_middle_here, 4, 4 * l)

    def part_arrived(layer):
        ref = parts.at[layer, pl.ds(4 * l, 8)]
        remote(leaving.at[0], ref, p_send.at[0], p_recv.at[layer], to_l).wait_recv()

    @pl.when(y == l)
    def _():
        part_arrived(l1)

    @pl.when(y != l)
    def _():
        part_arrived(0)
        part_arrived(1)

    remote(swapped, parts.at[l1, pl.ds(8 * l1, 4)], p_send.at[2], p_recv.at[2], to_l).wait_recv()

    def fill(owner, n):
        index = slot_source[owner * 6 + n]
        value = parts[0, index].astype(jnp.float32) + parts[1, index].astype(jnp.float32)
        slots[owner, n] = (value * slot_used[owner * 6 + n].astype(jnp.float32)).astype(jnp.bfloat16)

    def slot_copy(owner, n, index, device):
        return remote(
            slots.at[owner, n], out_ref.at[c, n], o_send.at[index, n], o_recv.at[index, n], device
        )

    targets = ((z2, to_z2, z2), (zp, to_zp, zm), (zm, to_zm, zp))

    def send_slots(n, inner):
        for index, (owner, device, _) in enumerate(targets):
            fill(owner, n)
            slot_copy(owner, n, index, device).start()
        return inner

    lax.fori_loop(0, 6, send_slots, 0)

    def keep_slots(n, inner):
        fill(c, n)
        return inner

    lax.fori_loop(0, 6, keep_slots, 0)
    stay = pltpu.make_async_copy(slots.at[c], out_ref.at[c], local_sem.at[5])
    stay.start()
    for phase in range(2):
        ref = abuf.at[phase, pl.ds(0, 15)]
        remote(ref, ref, a_send.at[phase], core_recv.at[phase, 0], to_b).wait_send()
    keep_copy.wait_send()
    b_full_over_y().wait_send()
    edges_over_y(r, lambda copy: copy.wait_send())

    def all_sent(part, inner):
        b_sent(part)
        return inner

    lax.fori_loop(0, 5, all_sent, 0)
    column_copy(0, to_other_column).wait_send()

    @pl.when(y != l)
    def _():
        column_copy(1, to_l).wait_send()

    middle_copy().wait_send()
    stay.wait()

    def end_slots(n, inner):
        for index, (owner, device, sender) in enumerate(targets):
            slot_copy(owner, n, index, device).wait_send()
            remote(
                slots.at[owner, n], out_ref.at[sender, n], o_send.at[index, n], o_recv.at[index, n], device
            ).wait_recv()
        return inner

    lax.fori_loop(0, 6, end_slots, 0)


def on_device(a_blocks, b_blocks, a_offsets, b_offsets, keep_offsets, owners):
    a_part = a_blocks.reshape(12, BLOCK, BLOCK)
    b_part = b_blocks.reshape(4, 8, BLOCK, BLOCK)
    keep = keep_offsets[:, 0, 0]
    smem = pl.BlockSpec(memory_space=pltpu.SMEM)
    anywhere = pl.BlockSpec(memory_space=pl.ANY)
    dma = pltpu.SemaphoreType.DMA
    block = (BLOCK, BLOCK)
    arrived = pl.pallas_call(
        kernel,
        out_shape=jax.ShapeDtypeStruct((4, 6, BLOCK, BLOCK), jnp.bfloat16),
        in_specs=[anywhere, anywhere, smem, smem, smem, smem, pl.BlockSpec(memory_space=pltpu.VMEM)],
        out_specs=anywhere,
        scratch_shapes=[
            pltpu.VMEM((2, 16, 4) + block, jnp.bfloat16),
            pltpu.VMEM((5, 4, 4) + block, jnp.bfloat16),
            pltpu.VMEM((8,) + block, jnp.float32),
            pltpu.VMEM((2, 12) + block, jnp.bfloat16),
            pltpu.VMEM((2, 8) + block, jnp.bfloat16),
            pltpu.VMEM((4,) + block, jnp.bfloat16),
            pltpu.VMEM((4, 6) + block, jnp.bfloat16),
            pltpu.VMEM((1, 24), jnp.int32),
            pltpu.SMEM((1, 24), jnp.int32),
            pltpu.SMEM((24,), jnp.int32),
            pltpu.SMEM((256,), jnp.int32),
            pltpu.SMEM((12,), jnp.int32),
            pltpu.SMEM((24,), jnp.int32),
            pltpu.SMEM((24,), jnp.int32),
            dma((7,)),
            dma((2,)),
            dma((2,)),
            dma((2,)),
            dma((2, 2, 2)),
            dma((2, 2, 2)),
            dma((2, 8)),
            dma((5,)),
            dma((5,)),
            dma((3, 5, 4)),
            dma((3, 5, 4)),
            dma((3,)),
            dma((3,)),
            dma((3, 6)),
            dma((3, 6)),
        ],
        compiler_params=pltpu.CompilerParams(
            collective_id=0, has_side_effects=True, vmem_limit_bytes=56 << 20
        ),
        cost_estimate=pl.CostEstimate(
            flops=192 * 2 * BLOCK**3, bytes_accessed=10 << 20, transcendentals=0
        ),
        name="banded_product",
    )(
        a_part,
        b_part,
        a_offsets.transpose(2, 1, 0),
        b_offsets.T,
        keep,
        owners[:, 0, 0],
        keep.reshape(1, 24),
    )
    return arrived.reshape(1, 1, 1, 4, 6, BLOCK, BLOCK)


def solution(mesh):
    return jax.shard_map(
        on_device,
        mesh=mesh,
        in_specs=(
            P("row", "col", "layer", None, None, None),
            P("row", "col", "layer", None, None, None),
            P(None, "col", None),
            P(),
            P(None, "col", "row"),
            P("layer", "col", "row"),
        ),
        out_specs=P("row", "col", "layer", None, None, None, None),
        check_vma=False,
    )
```

```python
import functools

import jax
import jax.numpy as jnp
from jax import lax
from jax.experimental import pallas as pl
from jax.experimental.pallas import tpu as pltpu
from jax.sharding import PartitionSpec as P

MESH = pl.DeviceIdType.MESH
BLOCK = 256


def mod(value, count):
    return lax.rem(value + 32 * count, jnp.int32(count))


def kernel(
    a_ref,
    b_ref,
    a_offsets,
    b_offsets,
    keep,
    owners,
    keep_vector,
    out_ref,
    abuf,
    bbuf,
    total,
    parts,
    leaving,
    swapped,
    slots,
    keep_arrived,
    keep_other,
    a_mask,
    b_mask,
    rank,
    slot_source,
    slot_used,
    local_sem,
    keep_sem,
    a_send,
    yy_recv,
    yx_recv,
    yx2_recv,
    core_recv,
    by_send,
    by_recv,
    bz_send,
    bz_recv,
    p_send,
    p_recv,
    o_send,
    o_recv,
):
    r = lax.axis_index("row")
    c = lax.axis_index("col")
    l = lax.axis_index("layer")
    x, y, b = r // 4, (r // 2) % 2, r % 2

    def row_of(xx, yy, bb):
        return xx * 4 + yy * 2 + bb

    xp, xm, x2 = mod(x + 1, 4), mod(x - 1, 4), mod(x + 2, 4)
    zp, zm, z2 = mod(c + 1, 4), mod(c - 1, 4), mod(c + 2, 4)
    y1, b1, l1 = 1 - y, 1 - b, 1 - l
    r1 = row_of(x, y1, b)
    to_xp, to_xm = {"row": row_of(xp, y, b)}, {"row": row_of(xm, y, b)}
    to_y, to_b = {"row": r1}, {"row": row_of(x, y, b1)}
    to_zp, to_zm, to_z2 = {"col": zp}, {"col": zm}, {"col": z2}
    to_l, to_yl = {"layer": l1}, {"row": r1, "layer": l1}

    barrier = pltpu.get_barrier_semaphore()
    for device in (to_xp, to_xm, to_y, to_b, to_zp, to_zm, to_z2, to_l, to_yl):
        pl.semaphore_signal(barrier, inc=1, device_id=device, device_id_type=MESH)
    pl.semaphore_wait(barrier, 9)

    def remote(src, dst, send, recv, device):
        return pltpu.make_async_remote_copy(
            src_ref=src, dst_ref=dst, send_sem=send, recv_sem=recv, device_id=device, device_id_type=MESH
        )

    def third(phase):
        return 2 * y if phase == 0 else 1

    def pass_a(source, phase, first, count, recv, device):
        ref = abuf.at[phase, source, pl.ds(first, count)]
        remote(ref, ref, a_send.at[phase], recv, device).start()

    def got_a(source, phase, first, count, recv):
        ref = abuf.at[phase, source, pl.ds(first, count)]
        remote(ref, ref, a_send.at[phase], recv, to_b).wait_recv()

    def own_copy(phase):
        return pltpu.make_async_copy(
            a_ref.at[pl.ds(third(phase) * 4, 4)], abuf.at[phase, r], local_sem.at[phase]
        )

    def a_to_y(phase):
        first = 8 * y1 if phase == 0 else 4
        remote(
            a_ref.at[pl.ds(first, 4)], abuf.at[phase, r], a_send.at[phase], yy_recv.at[phase], to_y
        ).start()

    def a_along_x(phase, yy):
        index = 0 if yy is y else 1
        s = row_of(x, yy, b)
        pass_a(s, phase, 0, 4, yx_recv.at[phase, index, 0], to_xp)
        pass_a(s, phase, 0, 4, yx_recv.at[phase, index, 1], to_xm)

    def a_further(phase, yy):
        index = 0 if yy is y else 1
        s = row_of(xm, yy, b)
        got_a(s, phase, 0, 4, yx_recv.at[phase, index, 0])
        pass_a(s, phase, 0, 2, yx2_recv.at[phase, index, 0], to_xp)
        s = row_of(xp, yy, b)
        got_a(s, phase, 0, 4, yx_recv.at[phase, index, 1])
        pass_a(s, phase, 2, 2, yx2_recv.at[phase, index, 1], to_xm)

    def to_sibling(phase, n):
        source = row_of(mod(x + n, 4), mod(y + n // 4, 2), b)
        pass_a(source, phase, 0, 4, core_recv.at[phase, n], to_b)

    def a_last(phase, yy):
        index = 0 if yy is y else 1
        s = row_of(x2, yy, b)
        got_a(s, phase, 0, 2, yx2_recv.at[phase, index, 0])
        got_a(s, phase, 2, 2, yx2_recv.at[phase, index, 1])

    other_full, other_edge = 3 + l, 4 - l
    own_second, own_last = 2 * y, 2 - 2 * y

    def b_own_copy(part):
        return pltpu.make_async_copy(
            b_ref.at[:, mod(y + part - l, 8)], bbuf.at[part, c], local_sem.at[2 + part]
        )

    def b_full_over_y():
        return remote(
            b_ref.at[:, mod(2 * y1, 8)], bbuf.at[other_full, c], by_send.at[4], by_recv.at[4], to_y
        )

    def b_edge_over_y(n):
        return remote(
            b_ref.at[n, mod(2 * y1 + 1 - 2 * l, 8)],
            bbuf.at[other_edge, c, n],
            by_send.at[n],
            by_recv.at[n],
            to_y,
        )

    def near(column, source, n):
        q = mod(column + 4 * source + n, 16)
        return jnp.where(l == 0, jnp.where(q <= 6, 1, 0), jnp.where(q >= 8, 1, 0))

    def edges_over_y(column, act):
        for n in range(4):

            @pl.when(near(column, c, n) == 1)
            def _():
                act(b_edge_over_y(n))

    def inside(part, source, n):
        column = jnp.where(part >= 3, r1, r)
        whole = jnp.where(part >= 3, jnp.where(part == other_full, 1, 0), jnp.where(part == 2 * l1, 0, 1))
        return whole + near(column, source, n) > 0

    def b_copy(part, source, n, way, device):
        ref = bbuf.at[part, source, n]
        return remote(ref, ref, bz_send.at[way, part, n], bz_recv.at[way, part, n], device)

    def b_start(part):
        for n in range(4):

            @pl.when(inside(part, c, n))
            def _():
                b_copy(part, c, n, 0, to_zp).start()
                b_copy(part, c, n, 1, to_zm).start()

    def b_further(part):
        for n in range(4):

            @pl.when(inside(part, zm, n))
            def _():
                b_copy(part, zm, n, 0, to_zp).wait_recv()
                if n < 2:
                    b_copy(part, zm, n, 2, to_zp).start()

            @pl.when(inside(part, zp, n))
            def _():
                b_copy(part, zp, n, 1, to_zm).wait_recv()
                if n >= 2:
                    b_copy(part, zp, n, 2, to_zm).start()

    def b_last(part):
        for n in range(4):

            @pl.when(inside(part, z2, n))
            def _():
                b_copy(part, z2, n, 2, to_zp).wait_recv()

    def b_sent(part):
        for n in range(4):

            @pl.when(inside(part, c, n))
            def _():
                b_copy(part, c, n, 0, to_zp).wait_send()
                b_copy(part, c, n, 1, to_zm).wait_send()

            @pl.when(inside(part, zm if n < 2 else zp, n))
            def _():
                b_copy(part, c, n, 2, to_zp).wait_send()

    def multiply(source, phase, column, keeps, first_part):
        piece = 16 * l + mod(source + 4 * c, 16)
        top = mod(piece - c + 8, 32) // 4
        for g in range(4):
            u = jnp.where(top >= 3, top - 3 + g, jnp.where(g <= top, g, g + 4))
            t = 8 * third(phase) + u
            i = c + 4 * t
            d = mod(piece - i + 8, 32) - 8
            k = mod(i + d, 256)
            part = mod(k // 32 + l, 8) + first_part
            e = mod(column - k + 8, 16) - 8
            distance = mod(k - column, 16)
            present = (
                lax.shift_right_logical(a_mask[t], d + 8) & lax.shift_right_logical(b_mask[k], e + 8) & 1
            )
            weight = jnp.where(keeps(t) == d + e, present, 0).astype(jnp.float32)
            product = jnp.dot(
                abuf[phase, source, g],
                bbuf[part, distance // 4, distance % 4],
                preferred_element_type=jnp.float32,
            )
            total[u] += product * weight

    def own_keep(t):
        return keep[t]

    def other_keep(t):
        return keep_other[0, t]

    def add_sources(phase, column, keeps, first_part, wait):
        total[...] = jnp.zeros_like(total)

        def of_this_core(n, inner):
            multiply(row_of(mod(x + n, 4), mod(y + n // 4, 2), b), phase, column, keeps, first_part)
            return inner

        lax.fori_loop(0, 8, of_this_core, 0)

        def of_sibling(n, inner):
            source = row_of(mod(x + n, 4), mod(y + n // 4, 2), b1)
            if wait:
                got_a(source, phase, 0, 4, core_recv.at[phase, n])
            multiply(source, phase, column, keeps, first_part)
            return inner

        lax.fori_loop(0, 8, of_sibling, 0)

    def add_middle(first, count):
        def place(at):
            early = at + jnp.where(at >= 2, 1, 0) + jnp.where(at >= 5, 1, 0)
            return jnp.where(at < 6, early, 4 * at - 22)

        def of_this_core(at, inner):
            n = place(at)
            source = row_of(mod(x + n, 4), mod(y + n // 4, 2), b)
            multiply(source, 1, r, own_keep, -y)
            return inner

        def of_sibling(at, inner):
            n = place(at)
            source = row_of(mod(x + n, 4), mod(y + n // 4, 2), b1)
            got_a(source, 1, 0, 4, core_recv.at[1, n])
            multiply(source, 1, r, own_keep, -y)
            return inner

        lax.fori_loop(first, first + count, of_this_core, 0)
        lax.fori_loop(first, first + count, of_sibling, 0)

    def store_rows(put, count, row):
        def one(n, inner):
            put(n, total[row + n].astype(jnp.bfloat16))
            return inner

        lax.fori_loop(0, count, one, 0)

    def column_copy(index, device):
        return remote(
            leaving.at[index],
            parts.at[l, pl.ds(4 * y, 8)],
            p_send.at[index],
            p_recv.at[l],
            device,
        )

    to_other_column = {"row": r1, "layer": y}

    def middle_copy():
        return remote(swapped, parts.at[l, pl.ds(8 * l, 4)], p_send.at[2], p_recv.at[2], to_l)

    def bits(offsets, at):
        found = jnp.int32(0)
        for n in range(12):
            found += lax.shift_left(jnp.int32(1), offsets(n, at) + 8)
        return found

    def plan():
        def a_row(t, inner):
            a_mask[t] = bits(lambda n, at: a_offsets[n, 0, at], t)
            return inner

        lax.fori_loop(0, 24, a_row, 0)

        def b_row(n, inner):
            k = mod(n - 8, 256)
            b_mask[k] = bits(lambda n, at: b_offsets[n, at], k)
            return inner

        lax.fori_loop(0, 111, b_row, 0)
        for t in range(12):
            before = jnp.int32(0)
            for n in range(t):
                before += jnp.where(owners[n] == owners[t], 1, 0)
            rank[t] = before

        def slot(at, inner):
            owner, place = at // 6, at % 6
            source, used = jnp.int32(0), jnp.int32(0)
            for t in range(12):
                here = jnp.where((owners[t] == owner) & (rank[t] == place), 1, 0)
                source += here * t
                used += here
            slot_source[at] = source
            slot_used[at] = used
            return inner

        lax.fori_loop(0, 24, slot, 0)

    own_copy(0).start()
    b_own_copy(1).start()
    b_own_copy(own_second).start()
    own_copy(1).start()
    b_own_copy(own_last).start()
    a_to_y(0)
    for index, device in ((0, to_xp), (1, to_xm)):
        remote(
            a_ref.at[pl.ds(8 * y, 4)], abuf.at[0, r], a_send.at[0], yx_recv.at[0, 0, index], device
        ).start()
    b_full_over_y().start()
    keep_copy = remote(keep_vector, keep_arrived, keep_sem.at[0], keep_sem.at[1], to_y)
    keep_copy.start()
    b_own_copy(1).wait()
    b_start(1)
    b_own_copy(own_second).wait()
    b_start(own_second)
    own_copy(0).wait()
    to_sibling(0, 0)
    plan()
    got_a(r1, 0, 0, 4, yy_recv.at[0])
    a_along_x(0, y1)
    own_copy(1).wait()
    a_along_x(1, y)
    edges_over_y(r, lambda copy: copy.start())
    b_full_over_y().wait_recv()
    b_start(other_full)
    a_to_y(1)
    to_sibling(0, 4)
    a_further(0, y)
    b_further(1)
    to_sibling(0, 1)
    to_sibling(0, 3)
    b_further(own_second)
    edges_over_y(r1, lambda copy: copy.wait_recv())
    b_start(other_edge)
    a_further(0, y1)
    to_sibling(0, 5)
    to_sibling(0, 7)
    got_a(r1, 1, 0, 4, yy_recv.at[1])
    a_along_x(1, y1)
    b_further(other_full)
    b_own_copy(own_last).wait()
    b_start(own_last)
    a_further(1, y)
    a_last(0, y)
    to_sibling(0, 2)
    a_last(0, y1)
    to_sibling(0, 6)
    to_sibling(1, 0)
    to_sibling(1, 4)
    b_last(1)
    b_last(own_second)
    b_further(other_edge)
    add_sources(0, r, own_keep, -y, True)

    @pl.when(y == l)
    def _():
        def put_here(n, value):
            parts[l, 4 * y + n] = value

        store_rows(put_here, 8, 0)

    @pl.when(y != l)
    def _():
        def put_own(n, value):
            leaving[1, n] = value

        store_rows(put_own, 8, 0)
        column_copy(1, to_l).start()

    to_sibling(1, 1)
    to_sibling(1, 3)
    a_further(1, y1)
    to_sibling(1, 5)
    to_sibling(1, 7)
    keep_copy.wait_recv()
    keep_local = pltpu.make_async_copy(keep_arrived, keep_other, local_sem.at[6])
    keep_local.start()
    keep_local.wait()
    b_last(other_full)
    b_last(other_edge)
    add_sources(0, r1, other_keep, 3 - 2 * y, False)

    def put_other(n, value):
        leaving[0, n] = value

    store_rows(put_other, 8, 0)
    column_copy(0, to_other_column).start()
    b_further(own_last)

    b_last(own_last)
    total[...] = jnp.zeros_like(total)
    add_middle(0, 6)
    a_last(1, y)
    to_sibling(1, 2)
    a_last(1, y1)
    to_sibling(1, 6)
    add_middle(6, 2)

    def put_middle(n, value):
        swapped[n] = value

    store_rows(put_middle, 4, 4 * l1)
    middle_copy().start()

    def put_middle_here(n, value):
        parts[l, 8 * l1 + n] = value

    store_rows(put_middle_here, 4, 4 * l)

    def part_arrived(layer):
        ref = parts.at[layer, pl.ds(4 * l, 8)]
        remote(leaving.at[0], ref, p_send.at[0], p_recv.at[layer], to_l).wait_recv()

    @pl.when(y == l)
    def _():
        part_arrived(l1)

    @pl.when(y != l)
    def _():
        part_arrived(0)
        part_arrived(1)

    remote(swapped, parts.at[l1, pl.ds(8 * l1, 4)], p_send.at[2], p_recv.at[2], to_l).wait_recv()

    def fill(owner, n):
        index = slot_source[owner * 6 + n]
        value = parts[0, index].astype(jnp.float32) + parts[1, index].astype(jnp.float32)
        slots[owner, n] = (value * slot_used[owner * 6 + n].astype(jnp.float32)).astype(jnp.bfloat16)

    def slot_copy(owner, n, index, device):
        return remote(
            slots.at[owner, n], out_ref.at[c, n], o_send.at[index, n], o_recv.at[index, n], device
        )

    targets = ((z2, to_z2, z2), (zp, to_zp, zm), (zm, to_zm, zp))

    def send_slots(n, inner):
        for index, (owner, device, _) in enumerate(targets):
            fill(owner, n)
            slot_copy(owner, n, index, device).start()
        return inner

    lax.fori_loop(0, 6, send_slots, 0)

    def keep_slots(n, inner):
        fill(c, n)
        return inner

    lax.fori_loop(0, 6, keep_slots, 0)
    stay = pltpu.make_async_copy(slots.at[c], out_ref.at[c], local_sem.at[5])
    stay.start()
    for phase in range(2):
        ref = abuf.at[phase, pl.ds(0, 15)]
        remote(ref, ref, a_send.at[phase], core_recv.at[phase, 0], to_b).wait_send()
    keep_copy.wait_send()
    b_full_over_y().wait_send()
    edges_over_y(r, lambda copy: copy.wait_send())

    def all_sent(part, inner):
        b_sent(part)
        return inner

    lax.fori_loop(0, 5, all_sent, 0)
    column_copy(0, to_other_column).wait_send()

    @pl.when(y != l)
    def _():
        column_copy(1, to_l).wait_send()

    middle_copy().wait_send()
    stay.wait()

    def end_slots(n, inner):
        for index, (owner, device, sender) in enumerate(targets):
            slot_copy(owner, n, index, device).wait_send()
            remote(
                slots.at[owner, n], out_ref.at[sender, n], o_send.at[index, n], o_recv.at[index, n], device
            ).wait_recv()
        return inner

    lax.fori_loop(0, 6, end_slots, 0)


def on_device(a_blocks, b_blocks, a_offsets, b_offsets, keep_offsets, owners):
    a_part = a_blocks.reshape(12, BLOCK, BLOCK)
    b_part = b_blocks.reshape(4, 8, BLOCK, BLOCK)
    keep = keep_offsets[:, 0, 0]
    smem = pl.BlockSpec(memory_space=pltpu.SMEM)
    anywhere = pl.BlockSpec(memory_space=pl.ANY)
    dma = pltpu.SemaphoreType.DMA
    block = (BLOCK, BLOCK)
    arrived = pl.pallas_call(
        kernel,
        out_shape=jax.ShapeDtypeStruct((4, 6, BLOCK, BLOCK), jnp.bfloat16),
        in_specs=[anywhere, anywhere, smem, smem, smem, smem, pl.BlockSpec(memory_space=pltpu.VMEM)],
        out_specs=anywhere,
        scratch_shapes=[
            pltpu.VMEM((2, 16, 4) + block, jnp.bfloat16),
            pltpu.VMEM((5, 4, 4) + block, jnp.bfloat16),
            pltpu.VMEM((8,) + block, jnp.float32),
            pltpu.VMEM((2, 12) + block, jnp.bfloat16),
            pltpu.VMEM((2, 8) + block, jnp.bfloat16),
            pltpu.VMEM((4,) + block, jnp.bfloat16),
            pltpu.VMEM((4, 6) + block, jnp.bfloat16),
            pltpu.VMEM((1, 24), jnp.int32),
            pltpu.SMEM((1, 24), jnp.int32),
            pltpu.SMEM((24,), jnp.int32),
            pltpu.SMEM((256,), jnp.int32),
            pltpu.SMEM((12,), jnp.int32),
            pltpu.SMEM((24,), jnp.int32),
            pltpu.SMEM((24,), jnp.int32),
            dma((7,)),
            dma((2,)),
            dma((2,)),
            dma((2,)),
            dma((2, 2, 2)),
            dma((2, 2, 2)),
            dma((2, 8)),
            dma((5,)),
            dma((5,)),
            dma((3, 5, 4)),
            dma((3, 5, 4)),
            dma((3,)),
            dma((3,)),
            dma((3, 6)),
            dma((3, 6)),
        ],
        compiler_params=pltpu.CompilerParams(
            collective_id=0, has_side_effects=True, vmem_limit_bytes=56 << 20
        ),
        cost_estimate=pl.CostEstimate(
            flops=192 * 2 * BLOCK**3, bytes_accessed=10 << 20, transcendentals=0
        ),
        name="banded_product",
    )(
        a_part,
        b_part,
        a_offsets.transpose(2, 1, 0),
        b_offsets.T,
        keep,
        owners[:, 0, 0],
        keep.reshape(1, 24),
    )
    return arrived.reshape(1, 1, 1, 4, 6, BLOCK, BLOCK)


def solution(mesh):
    return jax.shard_map(
        on_device,
        mesh=mesh,
        in_specs=(
            P("row", "col", "layer", None, None, None),
            P("row", "col", "layer", None, None, None),
            P(None, "col", None),
            P(),
            P(None, "col", "row"),
            P("layer", "col", "row"),
        ),
        out_specs=P("row", "col", "layer", None, None, None, None),
        check_vma=False,
    )
```
